512 devices in a mesh: group: 4 (over x), seq: 32 (over y_hi, z), tp: 4 (over y_lo, core).
Axes of the slice: x: 4, y: 4 (y_hi: 2, y_lo: 2; y = y_hi * 2 + y_lo), z: 16, core: 2. Of those that a mesh axis runs over, the one named last changes fastest.
Arguments:
- hidden: bfloat16 [32768, 5120], P(('group', 'seq')), may hold values from -6 to 6
- norm_gain: bfloat16 [5120], replicated, may hold values from 0.5 to 1.5
- gen_value: bfloat16 [5120, 2560], P('seq', 'tp'), may hold values from -0.078125 to 0.078125
- gen_head: bfloat16 [2560, 64], P('tp'), may hold values from -0.125 to 0.125
- critic_embed: bfloat16 [2, 64, 5120], replicated, may hold values from -0.75 to 0.75
- critic_gain: bfloat16 [2, 5120], replicated, may hold values from 0.5 to 1.5
- critic_value: bfloat16 [5120, 5120], P('seq', ('group', 'tp')), may hold values from -0.078125 to 0.078125
- critic_head: bfloat16 [5120, 64], P(('group', 'tp')), may hold values from -0.125 to 0.125
- noise: bfloat16 [32768, 64], P('seq'), may hold values from -6 to 6
- owner: int32 [32768], P(('group', 'seq')), may hold values from 0 to 32767, as said below
- tsteps: int32 [16], replicated, may hold values from 0 to 999
- noise_mix: float32 [2, 1000], replicated, may hold values from 0.3 to 1
- gap_weight: float32 [1000], replicated, may hold values from 2 to 16
Outputs:
- gen_latent: bfloat16 [32768, 64], P(('group', 'seq'))
- grad_hidden: bfloat16 [32768, 5120], P(('group', 'seq'), 'tp')
The draws below stay inside these ranges and needn't reach their ends.
Inputs may be any that keep to these rules, and one draw needn't show every extreme that they name: owner is a permutation of the token positions. The 256 tokens of one generator block (aligned blocks of 256) place at most 15 tokens in one critic position block (aligned blocks of 1024 positions), and exactly 15 in some; every critic position block receives tokens from every generator block.
All inputs are finite; a program needn't handle non-finite values.
Results may differ from the reference program's by a relative error of at most 0.035.
Values may be sent and summed in bfloat16 or wider, within the bound.
No kernel may reach another device: no remote copies, remote signals or barrier semaphores. Data moves between devices by JAX's collectives and lax.ppermute only.
A program may use at most 128 MiB of HBM per device.

```python
import math
import jax
import jax.numpy as jnp
from jax import lax

D = 5120
HW = 2560
C = 64
R = 256
FTOK = 2048
NT = 1000
TOKENS = 32768
FRAMES = 16
CRIT_ROWS = 1024
N_TP = 4


def draw_owner(key, part):
    key = jax.random.fold_in(key, 11)
    shards = TOKENS // R
    seq_count = TOKENS // CRIT_ROWS
    pair = R // seq_count
    spread = pair - 1
    key_src, key_dst, key_place, key_order = jax.random.split(key, 4)
    src_sign = jnp.where(jax.random.permutation(key_src, shards) < shards // 2, 1, -1)
    dst_sign = jnp.where(jax.random.permutation(key_dst, seq_count) < seq_count // 2, 1, -1)
    counts = pair + spread * src_sign[:, None] * dst_sign[None, :]
    inclusive = jnp.cumsum(counts, axis=1)
    exclusive = inclusive - counts
    below = jnp.cumsum(counts, axis=0) - counts
    ranks = jnp.arange(R)
    target = jnp.sum((inclusive[:, None, :] <= ranks[None, :, None]).astype(jnp.int32), axis=2)
    offset = jnp.take_along_axis(below, target, axis=1) + ranks[None, :] - jnp.take_along_axis(exclusive, target, axis=1)
    shuffles = jax.vmap(lambda k: jax.random.permutation(k, CRIT_ROWS))(jax.random.split(key_place, seq_count))
    position = target * CRIT_ROWS + shuffles[target, offset]
    orders = jax.vmap(lambda k: jax.random.permutation(k, R))(jax.random.split(key_order, shards))
    flat_index = (jnp.arange(shards)[:, None] * R + orders).reshape(-1)
    return jnp.zeros((TOKENS,), jnp.int32).at[flat_index].set(position.reshape(-1).astype(jnp.int32))


def place_ends(drawn, stream_key, low, top_value):
    spot = [jax.random.randint(jax.random.fold_in(stream_key, axis), (), 0, length) for axis, length in enumerate(drawn.shape)]
    longest = drawn.shape.index(max(drawn.shape))
    neighbour = spot[:longest] + [(spot[longest] + 1) % drawn.shape[longest]] + spot[longest + 1:]
    return drawn.at[tuple(spot)].set(low).at[tuple(neighbour)].set(top_value)


def level_of(key, shape, cuts, smallest, largest):
    level = 1.0
    for dim, blocks in cuts:
        heights = jax.random.uniform(jax.random.fold_in(jax.random.fold_in(key, 6), dim), (blocks,), jnp.float32, smallest / len(cuts), largest / len(cuts))
        level = level * jnp.repeat(jnp.exp(heights), shape[dim] // blocks).reshape((-1,) + (1,) * (len(shape) - 1 - dim))
    return level


def bell_draw(rng, shape, width, reach, pieces=(), held_as=jnp.bfloat16):
    array = jax.random.normal(rng, shape, jnp.float32) * width
    if len(pieces) > 0:
        array = level_of(rng, shape, pieces, -0.22, 0.18) * array
    return jnp.clip(array, min=-reach, max=reach).astype(held_as)


def setup_inputs(seed: int = 0) -> dict:
    seeds = jax.random.split(jax.random.key(seed), 14)
    return {
        "hidden": bell_draw(seeds[0], (TOKENS, D), 1.0, 6.0, ((0, 128),)),
        "norm_gain": jnp.clip(1.0 + 0.1 * jax.random.normal(seeds[1], (D,), jnp.float32), 0.5, 1.5).astype(jnp.bfloat16),
        "gen_value": bell_draw(seeds[2], (D, HW), D ** -0.5, 0.078125, ((0, 32), (1, 4))),
        "gen_head": bell_draw(seeds[3], (HW, C), HW ** -0.5, 0.125, ((0, 4),)),
        "critic_embed": bell_draw(seeds[4], (2, C, D), C ** -0.5, 0.75),
        "critic_gain": jnp.clip(1.0 + 0.1 * jax.random.normal(seeds[5], (2, D), jnp.float32), 0.5, 1.5).astype(jnp.bfloat16),
        "critic_value": bell_draw(seeds[6], (D, 2 * HW), D ** -0.5, 0.078125, ((0, 32), (1, 16))),
        "critic_head": bell_draw(seeds[7], (2 * HW, C), HW ** -0.5, 0.125, ((0, 16),)),
        "noise": bell_draw(seeds[8], (TOKENS, C), 1.0, 6.0, ((0, 32),)),
        "owner": draw_owner(jax.random.fold_in(seeds[13], 71), 0),
        "tsteps": place_ends(jax.random.randint(seeds[10], (FRAMES,), 0, NT), jax.random.fold_in(seeds[10], 1), 0, NT - 1).astype(jnp.int32),
        "noise_mix": jnp.clip(jax.random.uniform(seeds[11], (2, NT), jnp.float32, 0.3, 1.0), 0.3, 1.0),
        "gap_weight": jnp.clip(jnp.exp(jax.random.uniform(seeds[12], (NT,), jnp.float32, math.log(2.0), math.log(16.0))), 2.0, 16.0),
    }


def gelu_tanh(v):
    return jax.nn.gelu(v, approximate=True)

def reference(hidden, norm_gain, gen_value, gen_head, critic_embed, critic_gain, critic_value, critic_head, noise, owner, tsteps, noise_mix, gap_weight):
    block = math.gcd(TOKENS, 2048)
    count = TOKENS // block
    cols = HW // N_TP
    gain = norm_gain.astype(jnp.float32)

    def gen_forward(rows):
        inputs = rows.astype(jnp.float32)
        inverse = lax.rsqrt(lax.optimization_barrier(jnp.mean(inputs * inputs, axis=-1, keepdims=True)) + 1e-06)
        normed = (inputs * inverse * gain).astype(jnp.bfloat16)
        values = jnp.dot(normed, gen_value, preferred_element_type=jnp.float32)
        activated = gelu_tanh(values).astype(jnp.bfloat16)
        total = jnp.zeros((rows.shape[0], C), jnp.float32)
        for part in range(N_TP):
            term = jnp.dot(activated[:, part * cols:(part + 1) * cols], gen_head[part * cols:(part + 1) * cols], preferred_element_type=jnp.float32)
            total = total + lax.optimization_barrier(term.astype(jnp.bfloat16)).astype(jnp.float32)
        return (total.astype(jnp.bfloat16), values)
    latent, values = lax.map(gen_forward, hidden.reshape(count, block, D))
    gen_latent = latent.reshape(TOKENS, C)
    placed = jnp.zeros((TOKENS, C), jnp.float32).at[owner].set(gen_latent.astype(jnp.float32))
    frame_at = jnp.zeros((TOKENS,), jnp.int32).at[owner].set(jnp.arange(TOKENS, dtype=jnp.int32) // FTOK)
    level = tsteps[frame_at]
    signal_part = noise_mix[0][level][:, None]
    noise_part = noise_mix[1][level][:, None]
    weight = gap_weight[level][:, None]
    noisy = (signal_part * placed + noise_part * noise.astype(jnp.float32)).astype(jnp.bfloat16)

    def critic_pass(noisy_rows):
        outputs = []
        for which in range(2):
            embedded = jnp.dot(noisy_rows, critic_embed[which], preferred_element_type=jnp.float32)
            scale_rows = lax.rsqrt(lax.optimization_barrier(jnp.mean(embedded * embedded, axis=-1, keepdims=True)) + 1e-06)
            critic_normed = (embedded * scale_rows * critic_gain[which].astype(jnp.float32)).astype(jnp.bfloat16)
            critic_values = jnp.dot(critic_normed, critic_value[:, which * HW:(which + 1) * HW], preferred_element_type=jnp.float32)
            critic_act = gelu_tanh(critic_values).astype(jnp.bfloat16)
            outputs.append(jnp.dot(critic_act, critic_head[which * HW:(which + 1) * HW], preferred_element_type=jnp.float32))
        return outputs[1] - outputs[0]
    gap = lax.map(critic_pass, noisy.reshape(count, block, C)).reshape(TOKENS, C)
    pull = (weight * gap).astype(jnp.bfloat16)
    cotangent = pull[owner]

    def gen_backward(items):
        rows, vals, cot = items
        inputs = rows.astype(jnp.float32)
        inverse = lax.rsqrt(lax.optimization_barrier(jnp.mean(inputs * inputs, axis=-1, keepdims=True)) + 1e-06)
        grad_act = lax.dot_general(cot, gen_head, (((1,), (1,)), ((), ())), preferred_element_type=jnp.float32)
        gelu_back = jax.vjp(gelu_tanh, vals)[1]
        grad_values = gelu_back(grad_act)[0].astype(jnp.bfloat16)
        total = jnp.zeros((rows.shape[0], D), jnp.float32)
        for part in range(N_TP):
            term = lax.dot_general(grad_values[:, part * cols:(part + 1) * cols], gen_value[:, part * cols:(part + 1) * cols], (((1,), (1,)), ((), ())), preferred_element_type=jnp.float32)
            total = total + lax.optimization_barrier(term.astype(jnp.bfloat16)).astype(jnp.float32)
        scaled = total * gain
        mixed = lax.optimization_barrier(jnp.mean(inputs * scaled, axis=-1, keepdims=True))
        return (inverse * scaled - inputs * inverse * inverse * inverse * mixed).astype(jnp.bfloat16)
    grad_hidden = lax.map(gen_backward, (hidden.reshape(count, block, D), values.reshape(count, block, HW), cotangent.reshape(count, block, C)))
    return (gen_latent, grad_hidden.reshape(TOKENS, D))
```

```python
import jax
import jax.numpy as jnp
from jax import lax
from jax.sharding import PartitionSpec as P

FTOK = 2048
SLOTS = 16
F32 = jnp.float32
BF16 = jnp.bfloat16


def gelu_tanh(v):
    return jax.nn.gelu(v, approximate=True)


class Axis:
    def __init__(self, name, count, stride):
        self.name, self.count, self.stride = name, count, stride

    def index(self):
        return (lax.axis_index(self.name) // self.stride) % self.count

    def pairs(self, shift):
        size = lax.axis_size(self.name)
        out = []
        for i in range(size):
            mine = (i // self.stride) % self.count
            out.append((i, i + ((mine + shift) % self.count - mine) * self.stride))
        return out

    def send(self, x, shift):
        return lax.ppermute(x, self.name, self.pairs(shift))


def pick(x, i, dim):
    return lax.dynamic_index_in_dim(x, i, dim, keepdims=False)


def put(x, piece, i, dim):
    return lax.dynamic_update_index_in_dim(x, piece, i, dim)


def reduce_scatter(x, axis):
    me, n = axis.index(), axis.count
    total = pick(x, me, 0)
    for j in range(1, n):
        total = total + axis.send(pick(x, (me + j) % n, 0), j)
    return total


def gather(x, axis):
    me, n = axis.index(), axis.count
    out = put(jnp.zeros((n,) + x.shape, x.dtype), x, me, 0)
    for j in range(1, n):
        out = put(out, axis.send(x, j), (me - j) % n, 0)
    return out


def exchange(x, axis, dim):
    me, n = axis.index(), axis.count
    out = x
    for j in range(1, n):
        out = put(out, axis.send(pick(x, (me + j) % n, dim), j), (me - j) % n, dim)
    return out


def ring_gather(x, y_hi, z):
    rows = x.shape[0]
    n = z.count
    me_y, me_z = y_hi.index(), z.index()
    out = jnp.zeros((2 * n * rows,) + x.shape[1:], x.dtype)
    far = y_hi.send(x, 1)
    for piece, at_y in ((x, me_y), (far, 1 - me_y)):

        def place(out, part, at_z, skip=0):
            start = (at_y * n + at_z % n) * rows + skip
            return lax.dynamic_update_slice(out, part, (start, jnp.zeros_like(start)))

        out = place(out, piece, me_z)
        up = down = piece
        for step in range(1, n // 2):
            up, down = z.send(up, 1), z.send(down, -1)
            out = place(out, up, me_z - step)
            out = place(out, down, me_z + step)
        half = rows // 2
        out = place(out, z.send(up[:half], 1), me_z + n // 2)
        out = place(out, z.send(down[half:], -1), me_z + n // 2, half)
    return out


def local(
    hidden,
    norm_gain,
    gen_value,
    gen_head,
    critic_embed,
    critic_gain,
    critic_value,
    critic_head,
    noise,
    owner,
    tsteps,
    noise_mix,
    gap_weight,
):
    rows, width = hidden.shape
    latent_width = gen_head.shape[1]
    seq_count = lax.axis_size("seq")
    group_id, seq_id, tp_id = (lax.axis_index(a) for a in ("group", "seq", "tp"))
    shard_id = group_id * seq_count + seq_id
    n_z = seq_count // 2
    y_hi, z = Axis("seq", 2, n_z), Axis("seq", n_z, 1)
    z_hi, z_lo = Axis("seq", n_z // 4, 4), Axis("seq", 4, 1)
    y_lo, core = Axis("tp", 2, 2), Axis("tp", 2, 1)
    tp, group = Axis("tp", 4, 1), Axis("group", 4, 1)

    with jax.named_scope("gather_value"):
        gen_full = ring_gather(gen_value, y_hi, z)

    with jax.named_scope("critic_matrix"):
        depth, cols = critic_value.shape
        critic_id = group_id // 2
        embed = lax.dynamic_slice(
            critic_embed, (critic_id, 0, seq_id * depth), (1, latent_width, depth)
        )[0].astype(F32)
        scale = lax.dynamic_slice(critic_gain, (critic_id, seq_id * depth), (1, depth))
        part = jnp.dot(
            embed * scale.astype(F32),
            critic_value.astype(F32),
            precision=lax.Precision.HIGHEST,
        )
        each = latent_width // seq_count
        part = part.reshape(4, n_z // 4, 2, each, cols)
        part = reduce_scatter(part, z_lo)
        part = reduce_scatter(part, z_hi)
        part = reduce_scatter(part, y_hi)
        part = gather(part, z_hi)
        part = gather(part, y_hi)
        part = gather(part, z_lo)
        part = part.transpose(0, 2, 1, 3, 4).reshape(latent_width, cols)
        part = gather(gather(part, tp), group)
        matrix = part.transpose(2, 0, 1, 3).reshape(latent_width, 16 * cols)
        matrix_hi = matrix.astype(BF16)
        matrix_lo = (matrix - matrix_hi.astype(F32)).astype(BF16)
        matrix_two = jnp.concatenate([matrix_hi, matrix_lo], axis=0)

    with jax.named_scope("critic_head"):
        head = gather(gather(critic_head, tp), group)
        head = jnp.concatenate([-head[:2], head[2:]], axis=0).reshape(16 * cols, latent_width)

    with jax.named_scope("fetch_noise"):
        crit_rows = noise.shape[0]
        target = owner // crit_rows
        at = (target[:, None] == jnp.arange(seq_count, dtype=jnp.int32)[None, :]).astype(BF16)
        ids = jnp.arange(rows, dtype=jnp.int32)
        before = (ids[None, :] < ids[:, None]).astype(BF16)
        prefix = jnp.dot(before, at, preferred_element_type=F32)
        rank = jnp.sum(prefix * at.astype(F32), axis=1).astype(jnp.int32)
        slot = target * SLOTS + rank
        total = seq_count * SLOTS
        holds = jnp.arange(total, dtype=jnp.int32)[:, None] == slot[None, :]
        wanted = jnp.sum(jnp.where(holds, (owner % crit_rows + 1)[None, :], 0), axis=1) - 1
        wanted = wanted.reshape(2, n_z // 4, 4, SLOTS)
        wanted = exchange(exchange(exchange(wanted, z_lo, 2), z_hi, 1), y_hi, 0)
        take = wanted.reshape(total)[:, None] == jnp.arange(crit_rows, dtype=jnp.int32)[None, :]
        found = jnp.dot(take.astype(BF16), noise, preferred_element_type=F32).astype(BF16)
        found = found.reshape(2, n_z // 4, 4, SLOTS, latent_width)
        found = exchange(exchange(exchange(found, y_hi, 0), z_hi, 1), z_lo, 2)
        own_noise = lax.dot_general(
            holds.astype(BF16),
            found.reshape(total, latent_width),
            (((0,), (0,)), ((), ())),
            preferred_element_type=F32,
        )

    with jax.named_scope("levels"):
        level = tsteps[shard_id * rows // FTOK]
        signal_mix, noise_part = noise_mix[0, level], noise_mix[1, level] * own_noise
        weight = gap_weight[level]

    with jax.named_scope("forward"):
        inputs = hidden.astype(F32)
        inverse = lax.rsqrt(jnp.mean(inputs * inputs, axis=-1, keepdims=True) + 1e-06)
        normed = (inputs * inverse * norm_gain.astype(F32)).astype(BF16)
        values = jnp.dot(normed, gen_full, preferred_element_type=F32)
        activated, gelu_back = jax.vjp(gelu_tanh, values)
        latent_part = jnp.dot(activated.astype(BF16), gen_head, preferred_element_type=F32)
        parts = lax.all_gather(latent_part.astype(BF16), "tp", axis=0)
        gen_latent = jnp.sum(parts.astype(F32), axis=0).astype(BF16)
        slope = gelu_back(jnp.ones_like(values))[0]

    with jax.named_scope("critics"):
        noisy = (signal_mix * gen_latent.astype(F32) + noise_part).astype(BF16)
        scales = []
        for which in range(2):
            embedded = jnp.dot(noisy, critic_embed[which], preferred_element_type=F32)
            scales.append(
                lax.rsqrt(jnp.mean(embedded * embedded, axis=-1, keepdims=True) + 1e-06)
            )
        raw = jnp.dot(
            jnp.concatenate([noisy, noisy], axis=1), matrix_two, preferred_element_type=F32
        )
        half = raw.shape[1] // 2
        acts = jnp.concatenate(
            [
                gelu_tanh(raw[:, :half] * scales[0]).astype(BF16),
                gelu_tanh(raw[:, half:] * scales[1]).astype(BF16),
            ],
            axis=1,
        )
        gap = jnp.dot(acts, head, preferred_element_type=F32)
        cotangent = (weight * gap).astype(BF16)

    with jax.named_scope("backward"):
        grad_act = lax.dot_general(
            cotangent, gen_head, (((1,), (1,)), ((), ())), preferred_element_type=F32
        )
        grad_values = (slope * grad_act).astype(BF16)
        mixed = jnp.sum(grad_values.astype(F32) * values, axis=1)
        for j in range(1, 4):
            mixed = mixed + tp.send(jnp.sum(grad_values.astype(F32) * values, axis=1), j)
        columns = width // 4
        yl, c = y_lo.index(), core.index()

        def grad_slice(at_y, at_c):
            start = (at_y * 2 + at_c) * columns
            weights = lax.dynamic_slice_in_dim(gen_full, start, columns, 0)
            return lax.dot_general(
                grad_values, weights, (((1,), (1,)), ((), ())), preferred_element_type=F32
            )

        far = core.send(grad_slice(1 - yl, 1 - c).astype(BF16), 1)
        far = (grad_slice(1 - yl, c) + far.astype(F32)).astype(BF16)
        far = y_lo.send(far, 1)
        near = core.send(grad_slice(yl, 1 - c).astype(BF16), 1)
        near = grad_slice(yl, c) + near.astype(F32)
        grad_normed = near + far.astype(F32)
        first = tp_id * columns
        gain = lax.dynamic_slice_in_dim(norm_gain, first, columns, 0).astype(F32)
        own = lax.dynamic_slice_in_dim(hidden, first, columns, 1).astype(F32)
        pulled = inverse * inverse * (mixed / width)[:, None]
        grad_hidden = (inverse * (grad_normed * gain) - own * pulled).astype(BF16)
    return (gen_latent, grad_hidden)


def solution(mesh):
    return jax.shard_map(
        local,
        mesh=mesh,
        in_specs=(
            P(("group", "seq"), None),
            P(),
            P("seq", "tp"),
            P("tp", None),
            P(),
            P(),
            P("seq", ("group", "tp")),
            P(("group", "tp"), None),
            P("seq", None),
            P(("group", "seq")),
            P(),
            P(),
            P(),
        ),
        out_specs=(P(("group", "seq"), None), P(("group", "seq"), "tp")),
        check_vma=False,
    )
```

```python
import jax
import jax.numpy as jnp
from jax import lax
from jax.sharding import Mesh
from jax.sharding import PartitionSpec as P

FTOK = 2048
SLOTS = 16
LANES = 128
F32 = jnp.float32
BF16 = jnp.bfloat16
SEQ = ("y_hi", "z")
TP = ("y_lo", "core")
BLOCK = ("group",) + SEQ
SWAP = ((0, 1), (1, 0))


def gelu_tanh(v):
    return jax.nn.gelu(v, approximate=True)


def to_tiles(x, tiles):
    flat = jnp.pad(x, ((0, 0), (0, tiles * 8 * LANES - x.shape[1])))
    return flat.reshape(x.shape[0], tiles * 8, LANES)


def swap_all(x):
    return lax.all_to_all(x, SEQ, split_axis=0, concat_axis=0, tiled=True)


def local(
    hidden,
    norm_gain,
    gen_value,
    gen_head,
    critic_embed,
    critic_gain,
    critic_value,
    critic_head,
    noise,
    owner,
    tsteps,
    noise_mix,
    gap_weight,
):
    rows, width = hidden.shape
    latent_width = gen_head.shape[1]
    depth, gen_cols = gen_value.shape
    seq_count = lax.axis_size(SEQ)
    group_id, seq_id = lax.axis_index("group"), lax.axis_index(SEQ)
    yl, c = lax.axis_index("y_lo"), lax.axis_index("core")
    shard_id = lax.axis_index(BLOCK)

    with jax.named_scope("gather_value"):
        gen_pair = lax.all_gather(gen_value, "y_hi", axis=1, tiled=True)
        gen_full = lax.all_gather(gen_pair, "z", axis=0, tiled=True)

    with jax.named_scope("critic_matrix_part"):
        cols = critic_value.shape[1]
        critic_id = group_id // 2
        embed = lax.dynamic_slice(
            critic_embed, (critic_id, 0, seq_id * depth), (1, latent_width, depth)
        )[0].astype(F32)
        scale = lax.dynamic_slice(critic_gain, (critic_id, seq_id * depth), (1, depth))
        part = jnp.dot(
            embed * scale.astype(F32),
            critic_value.astype(F32),
            precision=lax.Precision.HIGHEST,
        )
        each = latent_width // seq_count
        part = part.reshape(seq_count, each * cols)

    with jax.named_scope("noise_requests"):
        crit_rows = noise.shape[0]
        target = owner // crit_rows
        at = (target[:, None] == jnp.arange(seq_count, dtype=jnp.int32)[None, :]).astype(BF16)
        ids = jnp.arange(rows, dtype=jnp.int32)
        before = (ids[None, :] < ids[:, None]).astype(BF16)
        prefix = jnp.dot(before, at, preferred_element_type=F32)
        rank = jnp.sum(prefix * at.astype(F32), axis=1).astype(jnp.int32)
        slot = target * SLOTS + rank
        total = seq_count * SLOTS
        holds = jnp.arange(total, dtype=jnp.int32)[:, None] == slot[None, :]
        wanted = jnp.sum(jnp.where(holds, (owner % crit_rows + 1)[None, :], 0), axis=1) - 1
        wanted = wanted.astype(F32).reshape(seq_count, SLOTS)

    with jax.named_scope("first_exchange"):
        sent = to_tiles(jnp.concatenate([part, wanted], axis=1), 1)
        got = swap_all(sent).reshape(seq_count, -1)

    with jax.named_scope("noise_replies"):
        asked = got[:, each * cols : each * cols + SLOTS].reshape(total)
        take = asked[:, None] == jnp.arange(crit_rows, dtype=jnp.int32).astype(F32)[None, :]
        found = jnp.dot(take.astype(BF16), noise, preferred_element_type=F32).astype(BF16)
        found = found.reshape(seq_count, SLOTS * latent_width)
        mine = jnp.sum(got[:, : each * cols], axis=0).astype(BF16)

    with jax.named_scope("second_exchange"):
        mine = jnp.broadcast_to(mine[None, :], (seq_count, each * cols))
        sent = to_tiles(jnp.concatenate([found, mine], axis=1), 2)
        got = swap_all(sent).reshape(seq_count, -1)
        found = got[:, : SLOTS * latent_width].reshape(total, latent_width)
        matrix = got[:, SLOTS * latent_width : SLOTS * latent_width + each * cols]
        matrix = matrix.reshape(latent_width, cols)
        own_noise = lax.dot_general(
            holds.astype(BF16), found, (((0,), (0,)), ((), ())), preferred_element_type=F32
        )

    with jax.named_scope("critic_gather"):
        matrix = lax.all_gather(matrix, ("group",) + TP, axis=1, tiled=True)
        head = jnp.where(critic_id == 1, critic_head, -critic_head)
        head = lax.all_gather(head, ("group",) + TP, axis=0, tiled=True)

    with jax.named_scope("levels"):
        level = tsteps[shard_id * rows // FTOK]
        signal_mix, noise_part = noise_mix[0, level], noise_mix[1, level] * own_noise
        weight = gap_weight[level]

    with jax.named_scope("forward"):
        inputs = hidden.astype(F32)
        inverse = lax.rsqrt(jnp.mean(inputs * inputs, axis=-1, keepdims=True) + 1e-06)
        normed = (inputs * inverse * norm_gain.astype(F32)).astype(BF16)
        half = width // 2
        values = jnp.dot(
            normed[:, :half], gen_full[:, :gen_cols], preferred_element_type=F32
        ) + jnp.dot(normed[:, half:], gen_full[:, gen_cols:], preferred_element_type=F32)
        activated, gelu_back = jax.vjp(gelu_tanh, values)
        latent_part = jnp.dot(activated.astype(BF16), gen_head, preferred_element_type=F32)
        parts = lax.all_gather(latent_part.astype(BF16), TP, axis=0)
        gen_latent = jnp.sum(parts.astype(F32), axis=0).astype(BF16)
        slope = gelu_back(jnp.ones_like(values))[0]

    with jax.named_scope("critics"):
        noisy = (signal_mix * gen_latent.astype(F32) + noise_part).astype(BF16)
        raw = jnp.dot(noisy, matrix, preferred_element_type=F32)
        split = raw.shape[1] // 2
        acts = []
        for which in range(2):
            embedded = jnp.dot(noisy, critic_embed[which], preferred_element_type=F32)
            scale_rows = lax.rsqrt(jnp.mean(embedded * embedded, axis=-1, keepdims=True) + 1e-06)
            own = raw[:, which * split : (which + 1) * split] * scale_rows
            acts.append(gelu_tanh(own).astype(BF16))
        gap = jnp.dot(jnp.concatenate(acts, axis=1), head, preferred_element_type=F32)
        cotangent = (weight * gap).astype(BF16)

    with jax.named_scope("backward"):
        grad_act = lax.dot_general(
            cotangent, gen_head, (((1,), (1,)), ((), ())), preferred_element_type=F32
        )
        grad_values = (slope * grad_act).astype(BF16)
        mixed = jnp.sum(grad_values.astype(F32) * values, axis=1)
        mixed = mixed + lax.ppermute(mixed, "core", SWAP)
        mixed = mixed + lax.ppermute(mixed, "y_lo", SWAP)
        columns = width // 4

        def grad_slice(at_y, at_c):
            weights = lax.dynamic_slice(
                gen_full, (at_c * columns, at_y * gen_cols), (columns, gen_cols)
            )
            return lax.dot_general(
                grad_values, weights, (((1,), (1,)), ((), ())), preferred_element_type=F32
            )

        far = lax.ppermute(grad_slice(1 - yl, 1 - c).astype(BF16), "core", SWAP)
        far = (grad_slice(1 - yl, c) + far.astype(F32)).astype(BF16)
        far = lax.ppermute(far, "y_lo", SWAP)
        near = lax.ppermute(grad_slice(yl, 1 - c).astype(BF16), "core", SWAP)
        near = grad_slice(yl, c) + near.astype(F32)
        grad_normed = near + far.astype(F32)
        first = (yl * 2 + c) * columns
        gain = lax.dynamic_slice_in_dim(norm_gain, first, columns, 0).astype(F32)
        own = lax.dynamic_slice_in_dim(hidden, first, columns, 1).astype(F32)
        pulled = inverse * inverse * (mixed / width)[:, None]
        grad_hidden = (inverse * (grad_normed * gain) - own * pulled).astype(BF16)
    return (gen_latent, grad_hidden)


def solution(mesh):
    shape = mesh.devices.shape
    fine = Mesh(
        mesh.devices.reshape(shape[0], 2, shape[1] // 2, 2, shape[2] // 2),
        ("group", "y_hi", "z", "y_lo", "core"),
    )
    return jax.shard_map(
        local,
        mesh=fine,
        in_specs=(
            P(BLOCK, None),
            P(),
            P(SEQ, TP),
            P(TP, None),
            P(),
            P(),
            P(SEQ, ("group",) + TP),
            P(("group",) + TP, None),
            P(SEQ, None),
            P(BLOCK),
            P(),
            P(),
            P(),
        ),
        out_specs=(P(BLOCK, None), P(BLOCK, TP)),
        check_vma=False,
    )
```

```python
import functools

import jax
import jax.numpy as jnp
from jax import lax
from jax.experimental import pallas as pl
from jax.experimental.pallas import tpu as pltpu
from jax.sharding import Mesh
from jax.sharding import PartitionSpec as P

FTOK = 2048
SLOTS = 16
LANES = 128
F32 = jnp.float32
BF16 = jnp.bfloat16
SEQ = ("y_hi", "z")
TP = ("y_lo", "core")
BLOCK = ("group",) + SEQ
SWAP = ((0, 1), (1, 0))


BUSY = 24 * 2**20
GELU_IN = 0.7978845608028654
GELU_CUBE = 0.044715
NT = (((1,), (1,)), ((), ()))


def twice_gelu(v):
    return v * (1.0 + jnp.tanh(v * (GELU_IN + (GELU_IN * GELU_CUBE) * (v * v))))


def whole(*shape):
    return pl.BlockSpec(shape, lambda *_: (0,) * len(shape))


def fetch(source, held, sems):
    count = sems.shape[0]
    deep = held.shape[0] // count
    copies = []
    for i in range(count):
        at = pl.ds(i * deep, deep)
        copies.append(pltpu.make_async_copy(source.at[at], held.at[at], sems.at[i]))
        copies[i].start()
    return copies


def forward_kernel(normed_ref, weights_ref, head_ref, slope_ref, part_ref, held, total, sems):
    copies = fetch(weights_ref, held, sems)
    steps = 4
    each = len(copies) // steps
    half, cols = held.shape[0], total.shape[1]
    deep = half // steps
    for step in range(steps):
        for copy in copies[step * each : (step + 1) * each]:
            copy.wait()
        first = slice(step * deep, (step + 1) * deep)
        second = slice(half + step * deep, half + (step + 1) * deep)
        term = jnp.dot(normed_ref[:, first], held[first, :cols], preferred_element_type=F32)
        term += jnp.dot(normed_ref[:, second], held[first, cols:], preferred_element_type=F32)
        if step == 0:
            total[...] = term
        else:
            total[...] += term
    v = total[...]
    square = v * v
    tanh = jnp.tanh(v * (GELU_IN + (GELU_IN * GELU_CUBE) * square))
    cdf = 0.5 + 0.5 * tanh
    bend = v * (1.0 - tanh * tanh) * (0.5 * GELU_IN + (1.5 * GELU_IN * GELU_CUBE) * square)
    slope = cdf + bend
    slope_ref[...] = slope
    head = head_ref[...]
    width = head.shape[1]
    part_ref[:, :width] = jnp.dot(
        (v * cdf).astype(BF16), head, preferred_element_type=F32
    ).astype(BF16)
    part_ref[:, width:] = jnp.dot(
        (v * slope).astype(BF16), head, preferred_element_type=F32
    ).astype(BF16)


def forward(normed, gen_full, gen_head):
    rows, width = normed.shape
    cols, latent_width = gen_head.shape
    vmem = pl.BlockSpec(memory_space=pltpu.VMEM)
    return pl.pallas_call(
        forward_kernel,
        in_specs=[vmem, pl.BlockSpec(memory_space=pltpu.HBM), vmem],
        out_specs=[vmem, vmem],
        out_shape=[
            jax.ShapeDtypeStruct((rows, cols), F32),
            jax.ShapeDtypeStruct((rows, 2 * latent_width), BF16),
        ],
        scratch_shapes=[
            pltpu.VMEM(gen_full.shape, BF16),
            pltpu.VMEM((rows, cols), F32),
            pltpu.SemaphoreType.DMA((8,)),
        ],
        compiler_params=pltpu.CompilerParams(vmem_limit_bytes=BUSY),
        cost_estimate=pl.CostEstimate(
            flops=2 * rows * width * cols, bytes_accessed=2 * width * cols, transcendentals=0
        ),
        name="forward",
    )(normed, gen_full, gen_head)


def block_at(ref, row, col, rows, cols):
    row = pl.multiple_of(row * rows, rows)
    col = pl.multiple_of(col * cols, cols)
    return ref.at[pl.ds(row, rows), pl.ds(col, cols)]


def store_slice(grad_values, held, copies, out_ref):
    deep = held.shape[0] // len(copies)
    for i, copy in enumerate(copies):
        copy.wait()
        at = slice(i * deep, (i + 1) * deep)
        out_ref[:, at] = lax.dot_general(
            grad_values, held[at, :], NT, preferred_element_type=F32
        ).astype(BF16)


def critic_kernel(
    width,
    place_ref,
    tsteps_ref,
    mix_ref,
    weight_ref,
    parts_ref,
    noise_ref,
    gram_ref,
    matrix_ref,
    head_ref,
    gen_head_ref,
    slope_ref,
    weights_ref,
    latent_ref,
    values_ref,
    mixed_ref,
    far_ref,
    held,
    sems,
):
    columns, cols = held.shape[1:]
    copies = []
    for i in range(2):
        source = block_at(weights_ref, place_ref[1 + 2 * i], place_ref[2 + 2 * i], columns, cols)
        copies.append(fetch(source, held.at[i], sems.at[i]))
    level = tsteps_ref[place_ref[0]]
    parts = parts_ref[...].astype(F32)
    parts = parts[0] + parts[1] + parts[2] + parts[3]
    latent_width = latent_ref.shape[1]
    latent = parts[:, :latent_width].astype(BF16)
    latent_ref[...] = latent
    noisy = mix_ref[0, level] * latent.astype(F32) + mix_ref[1, level] * noise_ref[...]
    noisy = noisy.astype(BF16)
    exact = noisy.astype(F32)
    rows = noisy.shape[0]
    scales = []
    for which in range(2):
        turned = jnp.dot(
            exact, gram_ref[which], precision=lax.Precision.HIGHEST, preferred_element_type=F32
        )
        square = jnp.sum(turned * exact, axis=1, keepdims=True) / width
        scales.append(lax.rsqrt(jnp.maximum(square, 0.0) + 1e-06))
    blocks = matrix_ref.shape[0]
    gap = jnp.zeros((rows, latent_width), F32)
    for i in range(blocks):
        own = jnp.dot(noisy, matrix_ref[i], preferred_element_type=F32)
        act = twice_gelu(own * scales[i * 2 // blocks]).astype(BF16)
        gap = gap + lax.dot_general(act, head_ref[i], NT, preferred_element_type=F32)
    cotangent = (weight_ref[0, level] * (0.5 * gap)).astype(BF16)
    cot = cotangent.astype(F32)
    mixed_ref[...] = jnp.sum(cot * parts[:, latent_width:], axis=1, keepdims=True)
    grad_act = lax.dot_general(cotangent, gen_head_ref[...], NT, preferred_element_type=F32)
    grad_values = (slope_ref[...] * grad_act).astype(BF16)
    values_ref[...] = grad_values
    for i in range(2):
        store_slice(grad_values, held.at[i], copies[i], far_ref.at[i])


def critics(width, place, tables, parts, own_noise, gram, matrix, head, gen_head, slope, gen_full):
    rows, cols = slope.shape
    latent_width = gen_head.shape[1]
    columns = gen_full.shape[0] // 2
    smem = pl.BlockSpec(memory_space=pltpu.SMEM)
    vmem = pl.BlockSpec(memory_space=pltpu.VMEM)
    return pl.pallas_call(
        functools.partial(critic_kernel, width),
        in_specs=[smem] * 4 + [vmem] * 7 + [pl.BlockSpec(memory_space=pltpu.HBM)],
        out_specs=[vmem] * 4,
        out_shape=[
            jax.ShapeDtypeStruct((rows, latent_width), BF16),
            jax.ShapeDtypeStruct((rows, cols), BF16),
            jax.ShapeDtypeStruct((rows, 1), F32),
            jax.ShapeDtypeStruct((2, rows, columns), BF16),
        ],
        scratch_shapes=[
            pltpu.VMEM((2, columns, cols), BF16),
            pltpu.SemaphoreType.DMA((2, 2)),
        ],
        compiler_params=pltpu.CompilerParams(vmem_limit_bytes=BUSY),
        name="critics",
    )(place, *tables, parts, own_noise, gram, matrix, head, gen_head, slope, gen_full)


def slices_kernel(place_ref, values_ref, weights_ref, out_ref, held, sems):
    columns, cols = held.shape[1:]
    copies = []
    for i in range(2):
        source = block_at(weights_ref, place_ref[2 * i], place_ref[2 * i + 1], columns, cols)
        copies.append(fetch(source, held.at[i], sems.at[i]))
    for i in range(2):
        store_slice(values_ref[...], held.at[i], copies[i], out_ref.at[i])


def grad_slices(place, grad_values, gen_full):
    rows, cols = grad_values.shape
    columns = gen_full.shape[0] // 2
    vmem = pl.BlockSpec(memory_space=pltpu.VMEM)
    return pl.pallas_call(
        slices_kernel,
        in_specs=[
            pl.BlockSpec(memory_space=pltpu.SMEM),
            vmem,
            pl.BlockSpec(memory_space=pltpu.HBM),
        ],
        out_specs=vmem,
        out_shape=jax.ShapeDtypeStruct((2, rows, columns), BF16),
        scratch_shapes=[
            pltpu.VMEM((2, columns, cols), BF16),
            pltpu.SemaphoreType.DMA((2, 2)),
        ],
        compiler_params=pltpu.CompilerParams(vmem_limit_bytes=BUSY),
        cost_estimate=pl.CostEstimate(
            flops=4 * rows * cols * columns,
            bytes_accessed=4 * cols * columns,
            transcendentals=0,
        ),
        name="grad_slices",
    )(place, grad_values, gen_full)


def finish_kernel(near_ref, far_ref, inverse_ref, gain_ref, out_ref):
    far = far_ref[...].astype(F32) * (inverse_ref[...] * gain_ref[...])
    out_ref[...] = (near_ref[...] + far).astype(BF16)


def finish(near, far, inverse, gain):
    rows, columns = near.shape
    steps = 2
    part = pl.BlockSpec((rows // steps, columns), lambda i: (i, 0))
    return pl.pallas_call(
        finish_kernel,
        grid=(steps,),
        in_specs=[
            part,
            part,
            pl.BlockSpec((rows // steps, 1), lambda i: (i, 0)),
            whole(1, columns),
        ],
        out_specs=part,
        out_shape=jax.ShapeDtypeStruct((rows, columns), BF16),
        compiler_params=pltpu.CompilerParams(vmem_limit_bytes=16 * 2**20),
        name="finish",
    )(near, far, inverse, gain)


def to_tiles(x, tiles):
    flat = jnp.pad(x, ((0, 0), (0, tiles * 8 * LANES - x.shape[1])))
    return flat.reshape(x.shape[0], tiles * 8, LANES)


def swap_all(x):
    return lax.all_to_all(x, SEQ, split_axis=0, concat_axis=0, tiled=True)


def local(
    hidden,
    norm_gain,
    gen_value,
    gen_head,
    critic_embed,
    critic_gain,
    critic_value,
    critic_head,
    noise,
    owner,
    tsteps,
    noise_mix,
    gap_weight,
):
    rows, width = hidden.shape
    latent_width = gen_head.shape[1]
    depth = gen_value.shape[0]
    seq_count = lax.axis_size(SEQ)
    group_id, seq_id = lax.axis_index("group"), lax.axis_index(SEQ)
    yl, c = lax.axis_index("y_lo"), lax.axis_index("core")
    shard_id = lax.axis_index(BLOCK)

    with jax.named_scope("gather_value"):
        gen_pair = lax.all_gather(gen_value, "y_hi", axis=1, tiled=True)
        gen_full = lax.all_gather(gen_pair, "z", axis=0, tiled=True)
        gen_full = pltpu.with_memory_space_constraint(gen_full, pltpu.HBM)

    with jax.named_scope("critic_matrix_part"):
        cols = critic_value.shape[1]
        critic_id = group_id // 2
        embed = lax.dynamic_slice(
            critic_embed, (critic_id, 0, seq_id * depth), (1, latent_width, depth)
        )[0].astype(F32)
        scale = lax.dynamic_slice(critic_gain, (critic_id, seq_id * depth), (1, depth))
        part = jnp.dot(
            embed * scale.astype(F32),
            critic_value.astype(F32),
            precision=lax.Precision.HIGHEST,
        )
        each = latent_width // seq_count
        part = part.reshape(seq_count, each * cols)

    with jax.named_scope("noise_requests"):
        crit_rows = noise.shape[0]
        target = owner // crit_rows
        at = (target[:, None] == jnp.arange(seq_count, dtype=jnp.int32)[None, :]).astype(BF16)
        ids = jnp.arange(rows, dtype=jnp.int32)
        before = (ids[None, :] < ids[:, None]).astype(BF16)
        prefix = jnp.dot(before, at, preferred_element_type=F32)
        rank = jnp.sum(prefix * at.astype(F32), axis=1).astype(jnp.int32)
        slot = target * SLOTS + rank
        total = seq_count * SLOTS
        holds = jnp.arange(total, dtype=jnp.int32)[:, None] == slot[None, :]
        wanted = jnp.sum(jnp.where(holds, (owner % crit_rows + 1)[None, :], 0), axis=1) - 1
        wanted = wanted.astype(F32).reshape(seq_count, SLOTS)

    with jax.named_scope("first_exchange"):
        sent = to_tiles(jnp.concatenate([part, wanted], axis=1), 1)
        got = swap_all(sent).reshape(seq_count, -1)

    with jax.named_scope("noise_replies"):
        asked = got[:, each * cols : each * cols + SLOTS].reshape(total)
        take = asked[:, None] == jnp.arange(crit_rows, dtype=jnp.int32).astype(F32)[None, :]
        found = jnp.dot(take.astype(BF16), noise, preferred_element_type=F32).astype(BF16)
        found = found.reshape(seq_count, SLOTS * latent_width)
        mine = jnp.sum(got[:, : each * cols], axis=0).astype(BF16)

    with jax.named_scope("second_exchange"):
        mine = jnp.broadcast_to(mine[None, :], (seq_count, each * cols))
        sent = to_tiles(jnp.concatenate([found, mine], axis=1), 2)
        got = swap_all(sent).reshape(seq_count, -1)
        found = got[:, : SLOTS * latent_width].reshape(total, latent_width)
        matrix = got[:, SLOTS * latent_width : SLOTS * latent_width + each * cols]
        matrix = matrix.reshape(latent_width, cols)
        own_noise = lax.dot_general(
            holds.astype(BF16), found, (((0,), (0,)), ((), ())), preferred_element_type=F32
        )

    with jax.named_scope("critic_gather"):
        matrix = lax.all_gather(matrix, ("group",) + TP, axis=0)
        head = jnp.where(critic_id == 1, critic_head, -critic_head).T
        head = lax.all_gather(head, ("group",) + TP, axis=0)
        gram = lax.dot_general(
            critic_embed, critic_embed, (((2,), (2,)), ((0,), (0,))), preferred_element_type=F32
        )

    with jax.named_scope("forward"):
        inputs = hidden.astype(F32)
        inverse = lax.rsqrt(jnp.mean(inputs * inputs, axis=-1, keepdims=True) + 1e-06)
        normed = (inputs * inverse * norm_gain.astype(F32)).astype(BF16)
        slope, part = forward(normed, gen_full, gen_head)
        parts = lax.all_gather(part, TP, axis=0)

    with jax.named_scope("critics"):
        frame = shard_id * rows // FTOK
        place = jnp.stack([frame, 1 - c, 1 - yl, 1 - c, yl]).astype(jnp.int32)
        tables = (tsteps, noise_mix, gap_weight[None, :])
        gen_latent, grad_values, mixed, far = critics(
            width,
            place,
            tables,
            parts,
            own_noise,
            gram,
            matrix,
            head,
            gen_head,
            slope,
            gen_full,
        )

    with jax.named_scope("backward"):
        columns = width // 4
        first = (yl * 2 + c) * columns
        gain = lax.dynamic_slice_in_dim(norm_gain, first, columns, 0).astype(F32)
        own = lax.dynamic_slice_in_dim(hidden, first, columns, 1).astype(F32)
        slope_out = inverse * gain[None, :]
        pulled = inverse * inverse * (mixed / width)
        got = lax.ppermute(far, "core", SWAP)
        places = jnp.stack([c, 1 - yl, c, yl])
        slices = grad_slices(places.astype(jnp.int32), grad_values, gen_full)
        far = (slices[0].astype(F32) + got[0].astype(F32)).astype(BF16)
        far, slices, got, pulled = lax.optimization_barrier((far, slices, got, pulled))
        far = lax.ppermute(far, "y_lo", SWAP)
        near = slices[1].astype(F32) + got[1].astype(F32)
        near = slope_out * near - own * pulled
        grad_hidden = finish(near, far, inverse, gain[None, :])
    return (gen_latent, grad_hidden)


def solution(mesh):
    shape = mesh.devices.shape
    fine = Mesh(
        mesh.devices.reshape(shape[0], 2, shape[1] // 2, 2, shape[2] // 2),
        ("group", "y_hi", "z", "y_lo", "core"),
    )
    return jax.shard_map(
        local,
        mesh=fine,
        in_specs=(
            P(BLOCK, None),
            P(),
            P(SEQ, TP),
            P(TP, None),
            P(),
            P(),
            P(SEQ, ("group",) + TP),
            P(("group",) + TP, None),
            P(SEQ, None),
            P(BLOCK),
            P(),
            P(),
            P(),
        ),
        out_specs=(P(BLOCK, None), P(BLOCK, TP)),
        check_vma=False,
    )
```

```python
import functools

import jax
import jax.numpy as jnp
from jax import lax
from jax.experimental import pallas as pl
from jax.experimental.pallas import tpu as pltpu
from jax.sharding import Mesh
from jax.sharding import PartitionSpec as P

FTOK = 2048
SLOTS = 16
LANES = 128
F32 = jnp.float32
BF16 = jnp.bfloat16
SEQ = ("y_hi", "z")
TP = ("y_lo", "core")
BLOCK = ("group",) + SEQ
SWAP = ((0, 1), (1, 0))


BUSY = 24 * 2**20
GELU_IN = 0.7978845608028654
GELU_CUBE = 0.044715
NT = (((1,), (1,)), ((), ()))


def twice_gelu(v):
    return v * (1.0 + jnp.tanh(v * (GELU_IN + (GELU_IN * GELU_CUBE) * (v * v))))


def whole(*shape):
    return pl.BlockSpec(shape, lambda *_: (0,) * len(shape))


def fetch(source, held, sems):
    count = sems.shape[0]
    deep = held.shape[0] // count
    copies = []
    for i in range(count):
        at = pl.ds(i * deep, deep)
        copies.append(pltpu.make_async_copy(source.at[at], held.at[at], sems.at[i]))
        copies[i].start()
    return copies


def forward_kernel(
    normed_ref, weights_ref, head_ref, slope_ref, part_ref, held, head_held, total, sems, head_sem
):
    copies = fetch(weights_ref, held, sems)
    head_copy = pltpu.make_async_copy(head_ref, head_held, head_sem)
    head_copy.start()
    steps = 4
    each = len(copies) // steps
    half, cols = held.shape[0], total.shape[1]
    deep = half // steps
    for step in range(steps):
        for copy in copies[step * each : (step + 1) * each]:
            copy.wait()
        first = slice(step * deep, (step + 1) * deep)
        second = slice(half + step * deep, half + (step + 1) * deep)
        term = jnp.dot(normed_ref[:, first], held[first, :cols], preferred_element_type=F32)
        term += jnp.dot(normed_ref[:, second], held[first, cols:], preferred_element_type=F32)
        if step == 0:
            total[...] = term
        else:
            total[...] += term
    v = total[...]
    square = v * v
    tanh = jnp.tanh(v * (GELU_IN + (GELU_IN * GELU_CUBE) * square))
    cdf = 0.5 + 0.5 * tanh
    bend = v * (1.0 - tanh * tanh) * (0.5 * GELU_IN + (1.5 * GELU_IN * GELU_CUBE) * square)
    slope = cdf + bend
    slope_ref[...] = slope
    head_copy.wait()
    head = head_held[...]
    width = head.shape[0]
    part_ref[:, :width] = lax.dot_general(
        (v * cdf).astype(BF16), head, NT, preferred_element_type=F32
    ).astype(BF16)
    part_ref[:, width:] = lax.dot_general(
        (v * slope).astype(BF16), head, NT, preferred_element_type=F32
    ).astype(BF16)


def forward(normed, gen_full, gen_head):
    rows, width = normed.shape
    latent_width, cols = gen_head.shape
    vmem = pl.BlockSpec(memory_space=pltpu.VMEM)
    hbm = pl.BlockSpec(memory_space=pltpu.HBM)
    return pl.pallas_call(
        forward_kernel,
        in_specs=[vmem, hbm, hbm],
        out_specs=[vmem, vmem, vmem],
        out_shape=[
            jax.ShapeDtypeStruct((rows, cols), F32),
            jax.ShapeDtypeStruct((rows, 2 * latent_width), BF16),
            jax.ShapeDtypeStruct(gen_full.shape, BF16),
        ],
        scratch_shapes=[
            pltpu.VMEM(gen_head.shape, BF16),
            pltpu.VMEM((rows, cols), F32),
            pltpu.SemaphoreType.DMA((8,)),
            pltpu.SemaphoreType.DMA,
        ],
        compiler_params=pltpu.CompilerParams(vmem_limit_bytes=BUSY),
        cost_estimate=pl.CostEstimate(
            flops=2 * rows * width * cols, bytes_accessed=2 * width * cols, transcendentals=0
        ),
        name="forward",
    )(normed, gen_full, gen_head)


def store_slice(grad_values, weights_ref, row, col, out_ref):
    rows, cols = out_ref.shape[1], grad_values.shape[1]
    col = pl.ds(pl.multiple_of(col * cols, cols), cols)
    parts = 2
    deep = rows // parts
    for i in range(parts):
        at = pl.ds(pl.multiple_of(row * rows + i * deep, deep), deep)
        out_ref[:, i * deep : (i + 1) * deep] = lax.dot_general(
            grad_values, weights_ref[at, col], NT, preferred_element_type=F32
        ).astype(BF16)


def critic_kernel(
    width,
    place_ref,
    tsteps_ref,
    mix_ref,
    weight_ref,
    parts_ref,
    noise_ref,
    gram_ref,
    matrix_ref,
    head_ref,
    gen_head_ref,
    slope_ref,
    weights_ref,
    latent_ref,
    mixed_ref,
    sent_ref,
    kept_ref,
):
    level = tsteps_ref[place_ref[0]]
    parts = parts_ref[...].astype(F32)
    parts = parts[0] + parts[1] + parts[2] + parts[3]
    latent_width = latent_ref.shape[1]
    latent = parts[:, :latent_width].astype(BF16)
    latent_ref[...] = latent
    noisy = mix_ref[0, level] * latent.astype(F32) + mix_ref[1, level] * noise_ref[...]
    noisy = noisy.astype(BF16)
    exact = noisy.astype(F32)
    rows = noisy.shape[0]
    scales = []
    for which in range(2):
        turned = jnp.dot(
            exact, gram_ref[which], precision=lax.Precision.HIGHEST, preferred_element_type=F32
        )
        square = jnp.sum(turned * exact, axis=1, keepdims=True) / width
        scales.append(lax.rsqrt(jnp.maximum(square, 0.0) + 1e-06))
    blocks = matrix_ref.shape[0]
    gap = jnp.zeros((rows, latent_width), F32)
    for i in range(blocks):
        own = jnp.dot(noisy, matrix_ref[i], preferred_element_type=F32)
        act = twice_gelu(own * scales[i * 2 // blocks]).astype(BF16)
        gap = gap + lax.dot_general(act, head_ref[i], NT, preferred_element_type=F32)
    cotangent = (weight_ref[0, level] * (0.5 * gap)).astype(BF16)
    cot = cotangent.astype(F32)
    mixed_ref[...] = jnp.sum(cot * parts[:, latent_width:], axis=1, keepdims=True)
    grad_act = jnp.dot(cotangent, gen_head_ref[...], preferred_element_type=F32)
    grad_values = (slope_ref[...] * grad_act).astype(BF16)
    for i in range(2):
        row, col = place_ref[1 + 2 * i], place_ref[2 + 2 * i]
        store_slice(grad_values, weights_ref, row, col, sent_ref.at[i])
    for i in range(2):
        row, col = place_ref[5 + 2 * i], place_ref[6 + 2 * i]
        store_slice(grad_values, weights_ref, row, col, kept_ref.at[i])


def critics(width, place, tables, parts, own_noise, gram, matrix, head, gen_head, slope, gen_full):
    rows, cols = slope.shape
    latent_width = gen_head.shape[0]
    columns = gen_full.shape[0] // 2
    smem = pl.BlockSpec(memory_space=pltpu.SMEM)
    vmem = pl.BlockSpec(memory_space=pltpu.VMEM)
    return pl.pallas_call(
        functools.partial(critic_kernel, width),
        in_specs=[smem] * 4 + [vmem] * 8,
        out_specs=[vmem] * 4,
        out_shape=[
            jax.ShapeDtypeStruct((rows, latent_width), BF16),
            jax.ShapeDtypeStruct((rows, 1), F32),
            jax.ShapeDtypeStruct((2, rows, columns), BF16),
            jax.ShapeDtypeStruct((2, rows, columns), BF16),
        ],
        compiler_params=pltpu.CompilerParams(vmem_limit_bytes=BUSY),
        name="critics",
    )(place, *tables, parts, own_noise, gram, matrix, head, gen_head, slope, gen_full)


def finish_kernel(near_ref, far_ref, inverse_ref, gain_ref, out_ref):
    far = far_ref[...].astype(F32) * (inverse_ref[...] * gain_ref[...])
    out_ref[...] = (near_ref[...] + far).astype(BF16)


def finish(near, far, inverse, gain):
    rows, columns = near.shape
    steps = 2
    part = pl.BlockSpec((rows // steps, columns), lambda i: (i, 0))
    return pl.pallas_call(
        finish_kernel,
        grid=(steps,),
        in_specs=[
            part,
            part,
            pl.BlockSpec((rows // steps, 1), lambda i: (i, 0)),
            whole(1, columns),
        ],
        out_specs=part,
        out_shape=jax.ShapeDtypeStruct((rows, columns), BF16),
        compiler_params=pltpu.CompilerParams(vmem_limit_bytes=16 * 2**20),
        name="finish",
    )(near, far, inverse, gain)


def to_tiles(x, tiles):
    flat = jnp.pad(x, ((0, 0), (0, tiles * 8 * LANES - x.shape[1])))
    return flat.reshape(x.shape[0], tiles * 8, LANES)


def swap_all(x):
    return lax.all_to_all(x, SEQ, split_axis=0, concat_axis=0, tiled=True)


def local(
    hidden,
    norm_gain,
    gen_value,
    gen_head,
    critic_embed,
    critic_gain,
    critic_value,
    critic_head,
    noise,
    owner,
    tsteps,
    noise_mix,
    gap_weight,
):
    rows, width = hidden.shape
    latent_width = gen_head.shape[1]
    depth = gen_value.shape[0]
    seq_count = lax.axis_size(SEQ)
    group_id, seq_id = lax.axis_index("group"), lax.axis_index(SEQ)
    yl, c = lax.axis_index("y_lo"), lax.axis_index("core")
    shard_id = lax.axis_index(BLOCK)

    with jax.named_scope("gather_value"):
        gen_pair = lax.all_gather(gen_value, "y_hi", axis=1, tiled=True)
        gen_full = lax.all_gather(gen_pair, "z", axis=0, tiled=True)
        gen_full = pltpu.with_memory_space_constraint(gen_full, pltpu.HBM)

    with jax.named_scope("critic_matrix_part"):
        cols = critic_value.shape[1]
        critic_id = group_id // 2
        embed = lax.dynamic_slice(
            critic_embed, (critic_id, 0, seq_id * depth), (1, latent_width, depth)
        )[0].astype(F32)
        scale = lax.dynamic_slice(critic_gain, (critic_id, seq_id * depth), (1, depth))
        part = jnp.dot(
            embed * scale.astype(F32),
            critic_value.astype(F32),
            precision=lax.Precision.HIGHEST,
        )
        each = latent_width // seq_count
        part = part.reshape(seq_count, each * cols)

    with jax.named_scope("noise_requests"):
        crit_rows = noise.shape[0]
        target = owner // crit_rows
        at = (target[:, None] == jnp.arange(seq_count, dtype=jnp.int32)[None, :]).astype(BF16)
        ids = jnp.arange(rows, dtype=jnp.int32)
        before = (ids[None, :] < ids[:, None]).astype(BF16)
        prefix = jnp.dot(before, at, preferred_element_type=F32)
        rank = jnp.sum(prefix * at.astype(F32), axis=1).astype(jnp.int32)
        slot = target * SLOTS + rank
        total = seq_count * SLOTS
        holds = jnp.arange(total, dtype=jnp.int32)[:, None] == slot[None, :]
        wanted = jnp.sum(jnp.where(holds, (owner % crit_rows + 1)[None, :], 0), axis=1) - 1
        wanted = wanted.astype(F32).reshape(seq_count, SLOTS)

    with jax.named_scope("first_exchange"):
        sent = to_tiles(jnp.concatenate([part, wanted], axis=1), 1)
        got = swap_all(sent).reshape(seq_count, -1)

    with jax.named_scope("noise_replies"):
        asked = got[:, each * cols : each * cols + SLOTS].reshape(total)
        take = asked[:, None] == jnp.arange(crit_rows, dtype=jnp.int32).astype(F32)[None, :]
        found = jnp.dot(take.astype(BF16), noise, preferred_element_type=F32).astype(BF16)
        found = found.reshape(seq_count, SLOTS * latent_width)
        mine = jnp.sum(got[:, : each * cols], axis=0).astype(BF16)

    with jax.named_scope("second_exchange"):
        mine = jnp.broadcast_to(mine[None, :], (seq_count, each * cols))
        sent = to_tiles(jnp.concatenate([found, mine], axis=1), 2)
        got = swap_all(sent).reshape(seq_count, -1)
        found = got[:, : SLOTS * latent_width].reshape(total, latent_width)
        matrix = got[:, SLOTS * latent_width : SLOTS * latent_width + each * cols]
        matrix = matrix.reshape(latent_width, cols)
        own_noise = lax.dot_general(
            holds.astype(BF16), found, (((0,), (0,)), ((), ())), preferred_element_type=F32
        )

    with jax.named_scope("critic_gather"):
        matrix = lax.all_gather(matrix, ("group",) + TP, axis=0)
        head = jnp.where(critic_id == 1, critic_head, -critic_head).T
        head = lax.all_gather(head, ("group",) + TP, axis=0)
        gram = lax.dot_general(
            critic_embed, critic_embed, (((2,), (2,)), ((0,), (0,))), preferred_element_type=F32
        )

    with jax.named_scope("forward"):
        inputs = hidden.astype(F32)
        inverse = lax.rsqrt(jnp.mean(inputs * inputs, axis=-1, keepdims=True) + 1e-06)
        normed = (inputs * inverse * norm_gain.astype(F32)).astype(BF16)
        head_turned = gen_head.T
        head_kept = pltpu.with_memory_space_constraint(head_turned, pltpu.HBM)
        slope, part, gen_full = forward(normed, gen_full, head_kept)
        parts = lax.all_gather(part, TP, axis=0)

    with jax.named_scope("critics"):
        frame = shard_id * rows // FTOK
        place = jnp.stack([frame, 1 - c, 1 - yl, 1 - c, yl, c, 1 - yl, c, yl]).astype(jnp.int32)
        tables = (tsteps, noise_mix, gap_weight[None, :])
        gen_latent, mixed, sent, kept = critics(
            width,
            place,
            tables,
            parts,
            own_noise,
            gram,
            matrix,
            head,
            head_turned,
            slope,
            gen_full,
        )

    with jax.named_scope("backward"):
        columns = width // 4
        first = (yl * 2 + c) * columns
        gain = lax.dynamic_slice_in_dim(norm_gain, first, columns, 0).astype(F32)
        own = lax.dynamic_slice_in_dim(hidden, first, columns, 1).astype(F32)
        slope_out = inverse * gain[None, :]
        pulled = inverse * inverse * (mixed / width)
        got = lax.ppermute(sent, "core", SWAP)
        far = (kept[0].astype(F32) + got[0].astype(F32)).astype(BF16)
        far, kept, got = lax.optimization_barrier((far, kept, got))
        far = lax.ppermute(far, "y_lo", SWAP)
        near = kept[1].astype(F32) + got[1].astype(F32)
        near = slope_out * near - own * pulled
        grad_hidden = finish(near, far, inverse, gain[None, :])
    return (gen_latent, grad_hidden)


def solution(mesh):
    shape = mesh.devices.shape
    fine = Mesh(
        mesh.devices.reshape(shape[0], 2, shape[1] // 2, 2, shape[2] // 2),
        ("group", "y_hi", "z", "y_lo", "core"),
    )
    return jax.shard_map(
        local,
        mesh=fine,
        in_specs=(
            P(BLOCK, None),
            P(),
            P(SEQ, TP),
            P(TP, None),
            P(),
            P(),
            P(SEQ, ("group",) + TP),
            P(("group",) + TP, None),
            P(SEQ, None),
            P(BLOCK),
            P(),
            P(),
            P(),
        ),
        out_specs=(P(BLOCK, None), P(BLOCK, TP)),
        check_vma=False,
    )
```

```python
import functools

import jax
import jax.numpy as jnp
from jax import lax
from jax.experimental import pallas as pl
from jax.experimental.pallas import tpu as pltpu
from jax.sharding import Mesh
from jax.sharding import PartitionSpec as P

FTOK = 2048
SLOTS = 16
LANES = 128
F32 = jnp.float32
BF16 = jnp.bfloat16
SEQ = ("y_hi", "z")
TP = ("y_lo", "core")
BLOCK = ("group",) + SEQ
SWAP = ((0, 1), (1, 0))


BUSY = 16 * 2**20
GELU_IN = 0.7978845608028654
GELU_CUBE = 0.044715
NT = (((1,), (1,)), ((), ()))


def twice_gelu(v):
    return v * (1.0 + jnp.tanh(v * (GELU_IN + (GELU_IN * GELU_CUBE) * (v * v))))


def whole(*shape):
    return pl.BlockSpec(shape, lambda *_: (0,) * len(shape))


def fetch(source, held, sems):
    count = sems.shape[0]
    deep = held.shape[0] // count
    copies = []
    for i in range(count):
        at = pl.ds(i * deep, deep)
        copies.append(pltpu.make_async_copy(source.at[at], held.at[at], sems.at[i]))
        copies[i].start()
    return copies


def forward_kernel(
    normed_ref, weights_ref, head_ref, slope_ref, part_ref, held, head_held, total, sems, head_sem
):
    copies = fetch(weights_ref, held, sems)
    head_copy = pltpu.make_async_copy(head_ref, head_held, head_sem)
    head_copy.start()
    steps = 4
    each = len(copies) // steps
    half, cols = held.shape[0], total.shape[1]
    deep = half // steps
    for step in range(steps):
        for copy in copies[step * each : (step + 1) * each]:
            copy.wait()
        first = slice(step * deep, (step + 1) * deep)
        second = slice(half + step * deep, half + (step + 1) * deep)
        term = jnp.dot(normed_ref[:, first], held[first, :cols], preferred_element_type=F32)
        term += jnp.dot(normed_ref[:, second], held[first, cols:], preferred_element_type=F32)
        if step == 0:
            total[...] = term
        else:
            total[...] += term
    v = total[...]
    square = v * v
    tanh = jnp.tanh(v * (GELU_IN + (GELU_IN * GELU_CUBE) * square))
    cdf = 0.5 + 0.5 * tanh
    bend = v * (1.0 - tanh * tanh) * (0.5 * GELU_IN + (1.5 * GELU_IN * GELU_CUBE) * square)
    slope = cdf + bend
    slope_ref[...] = slope
    head_copy.wait()
    head = head_held[...]
    width = head.shape[0]
    part_ref[:, :width] = lax.dot_general(
        (v * cdf).astype(BF16), head, NT, preferred_element_type=F32
    ).astype(BF16)
    part_ref[:, width:] = lax.dot_general(
        (v * slope).astype(BF16), head, NT, preferred_element_type=F32
    ).astype(BF16)


def forward(normed, gen_full, gen_head):
    rows, width = normed.shape
    latent_width, cols = gen_head.shape
    vmem = pl.BlockSpec(memory_space=pltpu.VMEM)
    hbm = pl.BlockSpec(memory_space=pltpu.HBM)
    return pl.pallas_call(
        forward_kernel,
        in_specs=[vmem, hbm, hbm],
        out_specs=[vmem, vmem, vmem],
        out_shape=[
            jax.ShapeDtypeStruct((rows, cols), F32),
            jax.ShapeDtypeStruct((rows, 2 * latent_width), BF16),
            jax.ShapeDtypeStruct(gen_full.shape, BF16),
        ],
        scratch_shapes=[
            pltpu.VMEM(gen_head.shape, BF16),
            pltpu.VMEM((rows, cols), F32),
            pltpu.SemaphoreType.DMA((8,)),
            pltpu.SemaphoreType.DMA,
        ],
        compiler_params=pltpu.CompilerParams(vmem_limit_bytes=BUSY),
        cost_estimate=pl.CostEstimate(
            flops=2 * rows * width * cols, bytes_accessed=2 * width * cols, transcendentals=0
        ),
        name="forward",
    )(normed, gen_full, gen_head)


def store_slice(grad_values, weights_ref, row, col, out_ref):
    rows, cols = out_ref.shape[1], grad_values.shape[1]
    col = pl.ds(pl.multiple_of(col * cols, cols), cols)
    parts = 2
    deep = rows // parts
    for i in range(parts):
        at = pl.ds(pl.multiple_of(row * rows + i * deep, deep), deep)
        out_ref[:, i * deep : (i + 1) * deep] = lax.dot_general(
            grad_values, weights_ref[at, col], NT, preferred_element_type=F32
        ).astype(BF16)


def critic_kernel(
    width,
    place_ref,
    tsteps_ref,
    mix_ref,
    weight_ref,
    parts_ref,
    noise_ref,
    gram_ref,
    matrix_ref,
    head_ref,
    gen_head_ref,
    slope_ref,
    weights_ref,
    latent_ref,
    mixed_ref,
    sent_ref,
    kept_ref,
):
    level = tsteps_ref[place_ref[0]]
    parts = parts_ref[...].astype(F32)
    parts = parts[0] + parts[1] + parts[2] + parts[3]
    latent_width = latent_ref.shape[1]
    latent = parts[:, :latent_width].astype(BF16)
    latent_ref[...] = latent
    noisy = mix_ref[0, level] * latent.astype(F32) + mix_ref[1, level] * noise_ref[...]
    noisy = noisy.astype(BF16)
    exact = noisy.astype(F32)
    rows = noisy.shape[0]
    scales = []
    for which in range(2):
        turned = jnp.dot(
            exact, gram_ref[which], precision=lax.Precision.HIGHEST, preferred_element_type=F32
        )
        square = jnp.sum(turned * exact, axis=1, keepdims=True) / width
        scales.append(lax.rsqrt(jnp.maximum(square, 0.0) + 1e-06))
    wide = 256
    count = matrix_ref.shape[1] // wide
    gap = jnp.zeros((rows, latent_width), F32)
    for i in range(count):
        at = slice(i * wide, (i + 1) * wide)
        own = jnp.dot(noisy, matrix_ref[:, at], preferred_element_type=F32)
        act = twice_gelu(own * scales[i * 2 // count]).astype(BF16)
        gap = gap + lax.dot_general(act, head_ref[:, at], NT, preferred_element_type=F32)
    cotangent = (weight_ref[0, level] * (0.5 * gap)).astype(BF16)
    cot = cotangent.astype(F32)
    mixed_ref[...] = jnp.sum(cot * parts[:, latent_width:], axis=1, keepdims=True)
    grad_act = jnp.dot(cotangent, gen_head_ref[...], preferred_element_type=F32)
    grad_values = (slope_ref[...] * grad_act).astype(BF16)
    for i in range(2):
        row, col = place_ref[1 + 2 * i], place_ref[2 + 2 * i]
        store_slice(grad_values, weights_ref, row, col, sent_ref.at[i])
    for i in range(2):
        row, col = place_ref[5 + 2 * i], place_ref[6 + 2 * i]
        store_slice(grad_values, weights_ref, row, col, kept_ref.at[i])


def critics(width, place, tables, parts, own_noise, gram, matrix, head, gen_head, slope, gen_full):
    rows, cols = slope.shape
    latent_width = gen_head.shape[0]
    columns = gen_full.shape[0] // 2
    smem = pl.BlockSpec(memory_space=pltpu.SMEM)
    vmem = pl.BlockSpec(memory_space=pltpu.VMEM)
    return pl.pallas_call(
        functools.partial(critic_kernel, width),
        in_specs=[smem] * 4 + [vmem] * 8,
        out_specs=[vmem] * 4,
        out_shape=[
            jax.ShapeDtypeStruct((rows, latent_width), BF16),
            jax.ShapeDtypeStruct((rows, 1), F32),
            jax.ShapeDtypeStruct((2, rows, columns), BF16),
            jax.ShapeDtypeStruct((2, rows, columns), BF16),
        ],
        compiler_params=pltpu.CompilerParams(vmem_limit_bytes=BUSY),
        name="critics",
    )(place, *tables, parts, own_noise, gram, matrix, head, gen_head, slope, gen_full)


def finish_kernel(near_ref, far_ref, inverse_ref, gain_ref, out_ref):
    far = far_ref[...].astype(F32) * (inverse_ref[...] * gain_ref[...])
    out_ref[...] = (near_ref[...] + far).astype(BF16)


def finish(near, far, inverse, gain):
    rows, columns = near.shape
    steps = 2
    part = pl.BlockSpec((rows // steps, columns), lambda i: (i, 0))
    return pl.pallas_call(
        finish_kernel,
        grid=(steps,),
        in_specs=[
            part,
            part,
            pl.BlockSpec((rows // steps, 1), lambda i: (i, 0)),
            whole(1, columns),
        ],
        out_specs=part,
        out_shape=jax.ShapeDtypeStruct((rows, columns), BF16),
        compiler_params=pltpu.CompilerParams(vmem_limit_bytes=16 * 2**20),
        name="finish",
    )(near, far, inverse, gain)


def unpack_kernel(got_ref, slot_ref, noise_ref, matrix_ref):
    got = got_ref[...]
    total, lanes = got.shape
    half = lanes // 2
    rows = slot_ref.shape[0]
    at = lax.broadcasted_iota(jnp.int32, (rows, total), 1)
    holds = jnp.where(at == slot_ref[...], 1.0, 0.0).astype(BF16)
    noise_ref[...] = jnp.dot(holds, got, preferred_element_type=F32)[:, :half]
    senders = total // SLOTS
    count = 2 * (matrix_ref.shape[1] // half)
    row = lax.broadcasted_iota(jnp.int32, (count * senders, total), 0)
    at = lax.broadcasted_iota(jnp.int32, (count * senders, total), 1)
    chosen = jnp.where(at == (row % senders) * SLOTS + row // senders, 1.0, 0.0).astype(BF16)
    parts = jnp.dot(chosen, got, preferred_element_type=F32).astype(BF16)
    for k in range(count):
        channel = k // (count // 2) * senders
        col = k % (count // 2) * half
        matrix_ref[channel : channel + senders, col : col + half] = parts[
            k * senders : (k + 1) * senders, half:
        ]


def unpack(got, slot, cols):
    rows = slot.shape[0]
    half = got.shape[1] // 2
    vmem = pl.BlockSpec(memory_space=pltpu.VMEM)
    return pl.pallas_call(
        unpack_kernel,
        in_specs=[vmem, vmem],
        out_specs=[vmem, vmem],
        out_shape=[
            jax.ShapeDtypeStruct((rows, half), F32),
            jax.ShapeDtypeStruct((half, cols), BF16),
        ],
        compiler_params=pltpu.CompilerParams(vmem_limit_bytes=16 * 2**20),
        name="unpack",
    )(got, slot)


def side_by_side(x):
    return x.transpose(1, 0, 2).reshape(x.shape[1], -1)


def swap_all(x):
    return lax.all_to_all(x, SEQ, split_axis=0, concat_axis=0, tiled=True)


def local(
    hidden,
    norm_gain,
    gen_value,
    gen_head,
    critic_embed,
    critic_gain,
    critic_value,
    critic_head,
    noise,
    owner,
    tsteps,
    noise_mix,
    gap_weight,
):
    rows, width = hidden.shape
    latent_width = gen_head.shape[1]
    depth = gen_value.shape[0]
    seq_count = lax.axis_size(SEQ)
    group_id, seq_id = lax.axis_index("group"), lax.axis_index(SEQ)
    yl, c = lax.axis_index("y_lo"), lax.axis_index("core")
    shard_id = lax.axis_index(BLOCK)

    with jax.named_scope("gather_value"):
        gen_pair = lax.all_gather(gen_value, "y_hi", axis=1, tiled=True)
        gen_full = lax.all_gather(gen_pair, "z", axis=0, tiled=True)
        gen_full = pltpu.with_memory_space_constraint(gen_full, pltpu.HBM)

    with jax.named_scope("critic_matrix_part"):
        cols = critic_value.shape[1]
        critic_id = group_id // 2
        embed = lax.dynamic_slice(
            critic_embed, (critic_id, 0, seq_id * depth), (1, latent_width, depth)
        )[0].astype(F32)
        scale = lax.dynamic_slice(critic_gain, (critic_id, seq_id * depth), (1, depth))
        part = jnp.dot(
            embed * scale.astype(F32),
            critic_value.astype(F32),
            precision=lax.Precision.HIGHEST,
        )
        quarter = LANES // 2
        wide = cols // quarter
        part = part.reshape(2, seq_count, wide, quarter).transpose(1, 2, 0, 3)
        part = part.reshape(seq_count, wide, LANES).astype(BF16)

    with jax.named_scope("noise_requests"):
        crit_rows = noise.shape[0]
        target = owner // crit_rows
        at = (target[:, None] == jnp.arange(seq_count, dtype=jnp.int32)[None, :]).astype(BF16)
        ids = jnp.arange(rows, dtype=jnp.int32)
        before = (ids[None, :] < ids[:, None]).astype(BF16)
        prefix = jnp.dot(before, at, preferred_element_type=F32)
        rank = jnp.sum(prefix * at.astype(F32), axis=1, keepdims=True).astype(jnp.int32)
        slot = target[:, None] * SLOTS + rank
        total = seq_count * SLOTS
        holds = jnp.arange(total, dtype=jnp.int32)[:, None] == slot[:, 0][None, :]
        wanted = jnp.sum(jnp.where(holds, (owner % crit_rows + 1)[None, :], 0), axis=1)
        wanted = wanted.reshape(seq_count, SLOTS)
        digits = [jnp.pad(d, ((0, 0), (0, quarter - SLOTS))) for d in (wanted // 32, wanted % 32)]
        digits = jnp.concatenate(digits, axis=1).astype(BF16)[:, None, :]

    with jax.named_scope("first_exchange"):
        sent = jnp.concatenate([part, digits], axis=1)
        sent = jnp.pad(sent, ((0, 0), (0, 8 - sent.shape[1]), (0, 0)))
        got = swap_all(sent)

    with jax.named_scope("noise_replies"):
        digits = got[:, wide].astype(F32)
        asked = (digits[:, :SLOTS] * 32 + digits[:, quarter : quarter + SLOTS]).reshape(total)
        take = asked[:, None] == jnp.arange(1, crit_rows + 1, dtype=jnp.int32).astype(F32)[None, :]
        found = jnp.dot(take.astype(BF16), noise, preferred_element_type=F32).astype(BF16)
        found = found.reshape(seq_count, SLOTS, latent_width)
        mine = jnp.sum(got[:, :wide].astype(F32), axis=0).astype(BF16)
        mine = jnp.concatenate([mine[:, :quarter], mine[:, quarter:]], axis=0)
        mine = jnp.pad(mine, ((0, SLOTS - mine.shape[0]), (0, 0)))

    with jax.named_scope("second_exchange"):
        mine = jnp.broadcast_to(mine[None], (seq_count, SLOTS, quarter))
        got = swap_all(jnp.concatenate([found, mine], axis=2))
        own_noise, matrix = unpack(got.reshape(total, LANES), slot, cols)

    with jax.named_scope("critic_gather"):
        matrix = side_by_side(lax.all_gather(matrix, ("group",) + TP, axis=0))
        head = jnp.where(critic_id == 1, critic_head, -critic_head).T
        head = side_by_side(lax.all_gather(head, ("group",) + TP, axis=0))
        gram = lax.dot_general(
            critic_embed, critic_embed, (((2,), (2,)), ((0,), (0,))), preferred_element_type=F32
        )

    with jax.named_scope("forward"):
        inputs = hidden.astype(F32)
        inverse = lax.rsqrt(jnp.mean(inputs * inputs, axis=-1, keepdims=True) + 1e-06)
        normed = (inputs * inverse * norm_gain.astype(F32)).astype(BF16)
        head_turned = gen_head.T
        head_kept = pltpu.with_memory_space_constraint(head_turned, pltpu.HBM)
        slope, part, gen_full = forward(normed, gen_full, head_kept)
        parts = lax.all_gather(part, TP, axis=0)

    with jax.named_scope("critics"):
        frame = shard_id * rows // FTOK
        place = jnp.stack([frame, 1 - c, 1 - yl, 1 - c, yl, c, 1 - yl, c, yl]).astype(jnp.int32)
        tables = (tsteps, noise_mix, gap_weight[None, :])
        gen_latent, mixed, sent, kept = critics(
            width,
            place,
            tables,
            parts,
            own_noise,
            gram,
            matrix,
            head,
            head_turned,
            slope,
            gen_full,
        )

    with jax.named_scope("backward"):
        columns = width // 4
        first = (yl * 2 + c) * columns
        gain = lax.dynamic_slice_in_dim(norm_gain, first, columns, 0).astype(F32)
        own = lax.dynamic_slice_in_dim(hidden, first, columns, 1).astype(F32)
        slope_out = inverse * gain[None, :]
        pulled = inverse * inverse * (mixed / width)
        got = lax.ppermute(sent, "core", SWAP)
        far = (kept[0].astype(F32) + got[0].astype(F32)).astype(BF16)
        far, kept, got = lax.optimization_barrier((far, kept, got))
        far = lax.ppermute(far, "y_lo", SWAP)
        near = kept[1].astype(F32) + got[1].astype(F32)
        near = slope_out * near - own * pulled
        grad_hidden = finish(near, far, inverse, gain[None, :])
    return (gen_latent, grad_hidden)


def solution(mesh):
    shape = mesh.devices.shape
    fine = Mesh(
        mesh.devices.reshape(shape[0], 2, shape[1] // 2, 2, shape[2] // 2),
        ("group", "y_hi", "z", "y_lo", "core"),
    )
    return jax.shard_map(
        local,
        mesh=fine,
        in_specs=(
            P(BLOCK, None),
            P(),
            P(SEQ, TP),
            P(TP, None),
            P(),
            P(),
            P(SEQ, ("group",) + TP),
            P(("group",) + TP, None),
            P(SEQ, None),
            P(BLOCK),
            P(),
            P(),
            P(),
        ),
        out_specs=(P(BLOCK, None), P(BLOCK, TP)),
        check_vma=False,
    )
```

```python
import functools

import jax
import jax.numpy as jnp
from jax import lax
from jax.experimental import pallas as pl
from jax.experimental.pallas import tpu as pltpu
from jax.sharding import Mesh
from jax.sharding import PartitionSpec as P

FTOK = 2048
SLOTS = 4
ROWS = 8
LANES = 128
F32 = jnp.float32
BF16 = jnp.bfloat16
SEQ = ("y_hi", "z")
TP = ("y_lo", "core")
BLOCK = ("group",) + SEQ
SWAP = ((0, 1), (1, 0))


BUSY = 16 * 2**20
GELU_IN = 0.7978845608028654
GELU_CUBE = 0.044715
NT = (((1,), (1,)), ((), ()))


def twice_gelu(v):
    return v * (1.0 + jnp.tanh(v * (GELU_IN + (GELU_IN * GELU_CUBE) * (v * v))))


def whole(*shape):
    return pl.BlockSpec(shape, lambda *_: (0,) * len(shape))


def fetch(source, held, sems):
    count = sems.shape[0]
    deep = held.shape[0] // count
    copies = []
    for i in range(count):
        at = pl.ds(i * deep, deep)
        copies.append(pltpu.make_async_copy(source.at[at], held.at[at], sems.at[i]))
        copies[i].start()
    return copies


def forward_kernel(
    normed_ref,
    weights_ref,
    head_ref,
    slope_ref,
    part_ref,
    held,
    head_held,
    total,
    sems,
    head_sem,
):
    copies = fetch(weights_ref, held, sems)
    head_copy = pltpu.make_async_copy(head_ref, head_held, head_sem)
    head_copy.start()
    steps = 10
    each = len(copies) // steps
    half, cols = held.shape[0], total.shape[1]
    deep = half // steps
    for step in range(steps):
        for copy in copies[step * each : (step + 1) * each]:
            copy.wait()
        first = slice(step * deep, (step + 1) * deep)
        second = slice(half + step * deep, half + (step + 1) * deep)
        term = jnp.dot(normed_ref[:, first], held[first, :cols], preferred_element_type=F32)
        term += jnp.dot(normed_ref[:, second], held[first, cols:], preferred_element_type=F32)
        if step == 0:
            total[...] = term
        else:
            total[...] += term
    v = total[...]
    square = v * v
    tanh = jnp.tanh(v * (GELU_IN + (GELU_IN * GELU_CUBE) * square))
    cdf = 0.5 + 0.5 * tanh
    bend = v * (1.0 - tanh * tanh) * (0.5 * GELU_IN + (1.5 * GELU_IN * GELU_CUBE) * square)
    slope = cdf + bend
    slope_ref[...] = slope
    head_copy.wait()
    head = head_held[...]
    width = head.shape[0]
    part_ref[:, :width] = lax.dot_general(
        (v * cdf).astype(BF16), head, NT, preferred_element_type=F32
    ).astype(BF16)
    part_ref[:, width:] = lax.dot_general(
        (v * slope).astype(BF16), head, NT, preferred_element_type=F32
    ).astype(BF16)


def forward(normed, gen_full, gen_head):
    rows, width = normed.shape
    latent_width, cols = gen_head.shape
    vmem = pl.BlockSpec(memory_space=pltpu.VMEM)
    hbm = pl.BlockSpec(memory_space=pltpu.HBM)
    return pl.pallas_call(
        forward_kernel,
        in_specs=[vmem, hbm, hbm],
        out_specs=[vmem] * 3,
        out_shape=[
            jax.ShapeDtypeStruct((rows, cols), F32),
            jax.ShapeDtypeStruct((rows, 2 * latent_width), BF16),
            jax.ShapeDtypeStruct(gen_full.shape, BF16),
        ],
        scratch_shapes=[
            pltpu.VMEM(gen_head.shape, BF16),
            pltpu.VMEM((rows, cols), F32),
            pltpu.SemaphoreType.DMA((20,)),
            pltpu.SemaphoreType.DMA,
        ],
        compiler_params=pltpu.CompilerParams(vmem_limit_bytes=BUSY),
        cost_estimate=pl.CostEstimate(
            flops=2 * rows * width * cols, bytes_accessed=2 * width * cols, transcendentals=0
        ),
        name="forward",
    )(normed, gen_full, gen_head)


def store_slice(grad_values, weights_ref, row, col, out_ref):
    rows, cols = out_ref.shape[1], grad_values.shape[1]
    col = pl.ds(pl.multiple_of(col * cols, cols), cols)
    parts = 2
    deep = rows // parts
    for i in range(parts):
        at = pl.ds(pl.multiple_of(row * rows + i * deep, deep), deep)
        out_ref[:, i * deep : (i + 1) * deep] = lax.dot_general(
            grad_values, weights_ref[at, col], NT, preferred_element_type=F32
        ).astype(BF16)


def critic_kernel(
    width,
    place_ref,
    tsteps_ref,
    mix_ref,
    weight_ref,
    parts_ref,
    noise_ref,
    gram_ref,
    matrix_ref,
    head_ref,
    gen_head_ref,
    slope_ref,
    weights_ref,
    latent_ref,
    mixed_ref,
    sent_ref,
    kept_ref,
):
    level = tsteps_ref[place_ref[0]]
    parts = parts_ref[...].astype(F32)
    parts = parts[0] + parts[1] + parts[2] + parts[3]
    latent_width = latent_ref.shape[1]
    latent = parts[:, :latent_width].astype(BF16)
    latent_ref[...] = latent
    noise = noise_ref[...].astype(F32)
    noise = noise[0] + noise[1] + noise[2] + noise[3]
    noisy = mix_ref[0, level] * latent.astype(F32) + mix_ref[1, level] * noise
    noisy = noisy.astype(BF16)
    exact = noisy.astype(F32)
    rows = noisy.shape[0]
    scales = []
    for which in range(2):
        turned = jnp.dot(
            exact, gram_ref[which], precision=lax.Precision.HIGHEST, preferred_element_type=F32
        )
        square = jnp.sum(turned * exact, axis=1, keepdims=True) / width
        scales.append(lax.rsqrt(jnp.maximum(square, 0.0) + 1e-06))
    wide = 256
    count = matrix_ref.shape[1] // wide
    gap = jnp.zeros((rows, latent_width), F32)
    for i in range(count):
        at = slice(i * wide, (i + 1) * wide)
        own = jnp.dot(noisy, matrix_ref[:, at], preferred_element_type=F32)
        act = twice_gelu(own * scales[i * 2 // count]).astype(BF16)
        gap = gap + lax.dot_general(act, head_ref[:, at], NT, preferred_element_type=F32)
    cotangent = (weight_ref[0, level] * (0.5 * gap)).astype(BF16)
    cot = cotangent.astype(F32)
    mixed_ref[...] = jnp.sum(cot * parts[:, latent_width:], axis=1, keepdims=True)
    grad_act = jnp.dot(cotangent, gen_head_ref[...], preferred_element_type=F32)
    grad_values = (slope_ref[...] * grad_act).astype(BF16)
    for i in range(2):
        row, col = place_ref[1 + 2 * i], place_ref[2 + 2 * i]
        store_slice(grad_values, weights_ref, row, col, sent_ref.at[i])
    for i in range(2):
        row, col = place_ref[5 + 2 * i], place_ref[6 + 2 * i]
        store_slice(grad_values, weights_ref, row, col, kept_ref.at[i])


def critics(width, place, tables, parts, own_noise, gram, matrix, head, gen_head, slope, gen_full):
    rows, cols = slope.shape
    latent_width = gen_head.shape[0]
    columns = gen_full.shape[0] // 2
    smem = pl.BlockSpec(memory_space=pltpu.SMEM)
    vmem = pl.BlockSpec(memory_space=pltpu.VMEM)
    return pl.pallas_call(
        functools.partial(critic_kernel, width),
        in_specs=[smem] * 4 + [vmem] * 8,
        out_specs=[vmem] * 4,
        out_shape=[
            jax.ShapeDtypeStruct((rows, latent_width), BF16),
            jax.ShapeDtypeStruct((rows, 1), F32),
            jax.ShapeDtypeStruct((2, rows, columns), BF16),
            jax.ShapeDtypeStruct((2, rows, columns), BF16),
        ],
        compiler_params=pltpu.CompilerParams(vmem_limit_bytes=BUSY),
        name="critics",
    )(place, *tables, parts, own_noise, gram, matrix, head, gen_head, slope, gen_full)


def finish_kernel(near_ref, far_ref, inverse_ref, gain_ref, out_ref):
    far = far_ref[...].astype(F32) * (inverse_ref[...] * gain_ref[...])
    out_ref[...] = (near_ref[...] + far).astype(BF16)


def finish(near, far, inverse, gain):
    rows, columns = near.shape
    steps = 2
    part = pl.BlockSpec((rows // steps, columns), lambda i: (i, 0))
    return pl.pallas_call(
        finish_kernel,
        grid=(steps,),
        in_specs=[
            part,
            part,
            pl.BlockSpec((rows // steps, 1), lambda i: (i, 0)),
            whole(1, columns),
        ],
        out_specs=part,
        out_shape=jax.ShapeDtypeStruct((rows, columns), BF16),
        compiler_params=pltpu.CompilerParams(vmem_limit_bytes=16 * 2**20),
        name="finish",
    )(near, far, inverse, gain)


def side_by_side_kernel(first_ref, second_ref, first_out, second_out):
    count, _, wide = first_ref.shape
    for i in range(count):
        first_out[:, i * wide : (i + 1) * wide] = first_ref[i]
        second_out[:, i * wide : (i + 1) * wide] = second_ref[i]


def side_by_side(first, second):
    count, rows, wide = first.shape
    vmem = pl.BlockSpec(memory_space=pltpu.VMEM)
    return pl.pallas_call(
        side_by_side_kernel,
        in_specs=[vmem, vmem],
        out_specs=[vmem, vmem],
        out_shape=[jax.ShapeDtypeStruct((rows, count * wide), BF16)] * 2,
        compiler_params=pltpu.CompilerParams(vmem_limit_bytes=BUSY),
        name="side_by_side",
    )(first, second)


def unpack_kernel(got_ref, slot_ref, noise_ref, matrix_ref):
    got = got_ref[...]
    total, lanes = got.shape
    half = lanes // 2
    rows = slot_ref.shape[0]
    at = lax.broadcasted_iota(jnp.int32, (rows, total), 1)
    holds = jnp.where(at == slot_ref[...], 1.0, 0.0).astype(BF16)
    noise_ref[...] = jnp.dot(holds, got, preferred_element_type=F32)[:, :half].astype(BF16)
    senders = total // ROWS
    count = 2 * (matrix_ref.shape[1] // half)
    row = lax.broadcasted_iota(jnp.int32, (count * senders, total), 0)
    at = lax.broadcasted_iota(jnp.int32, (count * senders, total), 1)
    piece = row // senders
    piece = jnp.where(piece < ROWS, piece, piece - ROWS + SLOTS)
    chosen = jnp.where(at == (row % senders) * ROWS + piece, 1.0, 0.0).astype(BF16)
    parts = jnp.dot(chosen, got, preferred_element_type=F32).astype(BF16)
    for k in range(count):
        channel = k // (count // 2) * senders
        col = k % (count // 2) * half
        side = half if k < ROWS else 0
        matrix_ref[channel : channel + senders, col : col + half] = parts[
            k * senders : (k + 1) * senders, side : side + half
        ]


def unpack(got, slot, cols):
    rows = slot.shape[0]
    half = got.shape[1] // 2
    vmem = pl.BlockSpec(memory_space=pltpu.VMEM)
    return pl.pallas_call(
        unpack_kernel,
        in_specs=[vmem, vmem],
        out_specs=[vmem, vmem],
        out_shape=[
            jax.ShapeDtypeStruct((rows, half), BF16),
            jax.ShapeDtypeStruct((half, cols), BF16),
        ],
        compiler_params=pltpu.CompilerParams(vmem_limit_bytes=16 * 2**20),
        name="unpack",
    )(got, slot)


def swap_all(x):
    return lax.all_to_all(x, SEQ, split_axis=0, concat_axis=0, tiled=True)


def local(
    hidden,
    norm_gain,
    gen_value,
    gen_head,
    critic_embed,
    critic_gain,
    critic_value,
    critic_head,
    noise,
    owner,
    tsteps,
    noise_mix,
    gap_weight,
):
    rows, width = hidden.shape
    latent_width = gen_head.shape[1]
    depth = gen_value.shape[0]
    seq_count = lax.axis_size(SEQ)
    group_id, seq_id = lax.axis_index("group"), lax.axis_index(SEQ)
    yl, c = lax.axis_index("y_lo"), lax.axis_index("core")
    shard_id = lax.axis_index(BLOCK)

    with jax.named_scope("gather_value"):
        gen_pair = lax.all_gather(gen_value, "y_hi", axis=1, tiled=True)
        gen_full = lax.all_gather(gen_pair, "z", axis=0, tiled=True)
        gen_full = pltpu.with_memory_space_constraint(gen_full, pltpu.HBM)

    with jax.named_scope("critic_matrix_part"):
        cols = critic_value.shape[1]
        critic_id = group_id // 2
        embed = lax.dynamic_slice(
            critic_embed, (critic_id, 0, seq_id * depth), (1, latent_width, depth)
        )[0].astype(F32)
        scale = lax.dynamic_slice(critic_gain, (critic_id, seq_id * depth), (1, depth))
        part = jnp.dot(
            embed * scale.astype(F32),
            critic_value.astype(F32),
            precision=lax.Precision.HIGHEST,
        )
        quarter = LANES // 2
        wide = cols // quarter
        part = part.reshape(2, seq_count, wide, quarter).transpose(1, 2, 0, 3)
        part = part.reshape(seq_count, wide, LANES).astype(BF16)

    with jax.named_scope("noise_requests"):
        crit_rows = noise.shape[0]
        target = owner // crit_rows
        at = (target[:, None] == jnp.arange(seq_count, dtype=jnp.int32)[None, :]).astype(BF16)
        ids = jnp.arange(rows, dtype=jnp.int32)
        before = (ids[None, :] < ids[:, None]).astype(BF16)
        prefix = jnp.dot(before, at, preferred_element_type=F32)
        rank = jnp.sum(prefix * at.astype(F32), axis=1, keepdims=True).astype(jnp.int32)
        mine_here = rank // SLOTS == yl * 2 + c
        slot = jnp.where(mine_here, target[:, None] * SLOTS + rank % SLOTS, -1)
        place_back = jnp.where(mine_here, target[:, None] * ROWS + rank % SLOTS, -1)
        total = seq_count * SLOTS
        holds = jnp.arange(total, dtype=jnp.int32)[:, None] == slot[:, 0][None, :]
        wanted = jnp.sum(jnp.where(holds, (owner % crit_rows + 1)[None, :], 0), axis=1)
        wanted = wanted.reshape(seq_count, SLOTS)
        digits = [jnp.pad(d, ((0, 0), (0, quarter - SLOTS))) for d in (wanted // 32, wanted % 32)]
        digits = jnp.concatenate(digits, axis=1).astype(BF16)[:, None, :]

    with jax.named_scope("first_exchange"):
        sent = jnp.concatenate([part, digits], axis=1)
        sent = jnp.pad(sent, ((0, 0), (0, 8 - sent.shape[1]), (0, 0)))
        gram = lax.dot_general(
            critic_embed, critic_embed, (((2,), (2,)), ((0,), (0,))), preferred_element_type=F32
        )
        got, gram = lax.optimization_barrier((swap_all(sent), gram))

    with jax.named_scope("noise_replies"):
        digits = got[:, wide].astype(F32)
        asked = (digits[:, :SLOTS] * 32 + digits[:, quarter : quarter + SLOTS]).reshape(total)
        take = asked[:, None] == jnp.arange(1, crit_rows + 1, dtype=jnp.int32).astype(F32)[None, :]
        found = jnp.dot(take.astype(BF16), noise, preferred_element_type=F32).astype(BF16)
        found = found.reshape(seq_count, SLOTS, latent_width)
        mine = jnp.sum(got[:, :wide].astype(F32), axis=0).astype(BF16)
        mine = jnp.concatenate([mine[:, :quarter], mine[:, quarter:]], axis=0)
        left = jnp.pad(mine[ROWS:], ((0, ROWS - SLOTS - (mine.shape[0] - ROWS)), (0, 0)))

    with jax.named_scope("second_exchange"):
        left = jnp.broadcast_to(left[None], (seq_count, ROWS - SLOTS, quarter))
        right = jnp.broadcast_to(mine[None, :ROWS], (seq_count, ROWS, quarter))
        sent = jnp.concatenate([jnp.concatenate([found, left], axis=1), right], axis=2)
        got = swap_all(sent)
        own_noise, matrix = unpack(got.reshape(seq_count * ROWS, LANES), place_back, cols)

    with jax.named_scope("critic_gather"):
        noise_parts = lax.all_gather(own_noise, TP, axis=0)
        matrices = lax.all_gather(matrix, ("group",) + TP, axis=0)
        head = jnp.where(critic_id == 1, critic_head, -critic_head).T
        heads = lax.all_gather(head, ("group",) + TP, axis=0)
        matrix, head = side_by_side(matrices, heads)

    with jax.named_scope("forward"):
        inputs = hidden.astype(F32)
        inverse = lax.rsqrt(jnp.mean(inputs * inputs, axis=-1, keepdims=True) + 1e-06)
        normed = (inputs * inverse * norm_gain.astype(F32)).astype(BF16)
        head_turned = gen_head.T
        head_kept = pltpu.with_memory_space_constraint(head_turned, pltpu.HBM)
        slope, part, gen_full = forward(normed, gen_full, head_kept)
        parts = lax.all_gather(part, TP, axis=0)

    with jax.named_scope("critics"):
        frame = shard_id * rows // FTOK
        place = jnp.stack([frame, 1 - c, 1 - yl, 1 - c, yl, c, 1 - yl, c, yl]).astype(jnp.int32)
        tables = (tsteps, noise_mix, gap_weight[None, :])
        gen_latent, mixed, sent, kept = critics(
            width,
            place,
            tables,
            parts,
            noise_parts,
            gram,
            matrix,
            head,
            head_turned,
            slope,
            gen_full,
        )

    with jax.named_scope("backward"):
        columns = width // 4
        first = (yl * 2 + c) * columns
        gain = lax.dynamic_slice_in_dim(norm_gain, first, columns, 0).astype(F32)
        own = lax.dynamic_slice_in_dim(hidden, first, columns, 1).astype(F32)
        slope_out = inverse * gain[None, :]
        pulled = inverse * inverse * (mixed / width)
        got = lax.ppermute(sent, "core", SWAP)
        far = (kept[0].astype(F32) + got[0].astype(F32)).astype(BF16)
        far, kept, got = lax.optimization_barrier((far, kept, got))
        far = lax.ppermute(far, "y_lo", SWAP)
        near = kept[1].astype(F32) + got[1].astype(F32)
        near = slope_out * near - own * pulled
        grad_hidden = finish(near, far, inverse, gain[None, :])
    return (gen_latent, grad_hidden)


def solution(mesh):
    shape = mesh.devices.shape
    fine = Mesh(
        mesh.devices.reshape(shape[0], 2, shape[1] // 2, 2, shape[2] // 2),
        ("group", "y_hi", "z", "y_lo", "core"),
    )
    return jax.shard_map(
        local,
        mesh=fine,
        in_specs=(
            P(BLOCK, None),
            P(),
            P(SEQ, TP),
            P(TP, None),
            P(),
            P(),
            P(SEQ, ("group",) + TP),
            P(("group",) + TP, None),
            P(SEQ, None),
            P(BLOCK),
            P(),
            P(),
            P(),
        ),
        out_specs=(P(BLOCK, None), P(BLOCK, TP)),
        check_vma=False,
    )
```

```python
import functools

import jax
import jax.numpy as jnp
from jax import lax
from jax.experimental import pallas as pl
from jax.experimental.pallas import tpu as pltpu
from jax.sharding import Mesh
from jax.sharding import PartitionSpec as P

FTOK = 2048
SLOTS = 4
ROWS = 8
LANES = 128
F32 = jnp.float32
BF16 = jnp.bfloat16
SEQ = ("y_hi", "z")
TP = ("y_lo", "core")
BLOCK = ("group",) + SEQ
SWAP = ((0, 1), (1, 0))


BUSY = 16 * 2**20
GELU_IN = 0.7978845608028654
GELU_CUBE = 0.044715
NT = (((1,), (1,)), ((), ()))


def twice_gelu(v):
    return v * (1.0 + jnp.tanh(v * (GELU_IN + (GELU_IN * GELU_CUBE) * (v * v))))


def whole(*shape):
    return pl.BlockSpec(shape, lambda *_: (0,) * len(shape))


def fetch(source, held, sems):
    count = sems.shape[0]
    deep = held.shape[0] // count
    copies = []
    for i in range(count):
        at = pl.ds(i * deep, deep)
        copies.append(pltpu.make_async_copy(source.at[at], held.at[at], sems.at[i]))
        copies[i].start()
    return copies


def forward_kernel(
    normed_ref,
    weights_ref,
    head_ref,
    slope_ref,
    part_ref,
    held,
    head_held,
    total,
    sems,
    head_sem,
):
    copies = fetch(weights_ref, held, sems)
    head_copy = pltpu.make_async_copy(head_ref, head_held, head_sem)
    head_copy.start()
    steps = 4
    each = len(copies) // steps
    half, cols = held.shape[0], total.shape[1]
    deep = half // steps
    for step in range(steps):
        for copy in copies[step * each : (step + 1) * each]:
            copy.wait()
        first = slice(step * deep, (step + 1) * deep)
        second = slice(half + step * deep, half + (step + 1) * deep)
        term = jnp.dot(normed_ref[:, first], held[first, :cols], preferred_element_type=F32)
        term += jnp.dot(normed_ref[:, second], held[first, cols:], preferred_element_type=F32)
        if step == 0:
            total[...] = term
        else:
            total[...] += term
    v = total[...]
    square = v * v
    tanh = jnp.tanh(v * (GELU_IN + (GELU_IN * GELU_CUBE) * square))
    cdf = 0.5 + 0.5 * tanh
    bend = v * (1.0 - tanh * tanh) * (0.5 * GELU_IN + (1.5 * GELU_IN * GELU_CUBE) * square)
    slope = cdf + bend
    slope_ref[...] = slope
    head_copy.wait()
    head = head_held[...]
    width = head.shape[0]
    part_ref[:, :width] = lax.dot_general(
        (v * cdf).astype(BF16), head, NT, preferred_element_type=F32
    ).astype(BF16)
    part_ref[:, width:] = lax.dot_general(
        (v * slope).astype(BF16), head, NT, preferred_element_type=F32
    ).astype(BF16)


def forward(normed, gen_full, gen_head):
    rows, width = normed.shape
    latent_width, cols = gen_head.shape
    vmem = pl.BlockSpec(memory_space=pltpu.VMEM)
    hbm = pl.BlockSpec(memory_space=pltpu.HBM)
    return pl.pallas_call(
        forward_kernel,
        in_specs=[vmem, hbm, hbm],
        out_specs=[vmem] * 3,
        out_shape=[
            jax.ShapeDtypeStruct((rows, cols), F32),
            jax.ShapeDtypeStruct((rows, 2 * latent_width), BF16),
            jax.ShapeDtypeStruct(gen_full.shape, BF16),
        ],
        scratch_shapes=[
            pltpu.VMEM(gen_head.shape, BF16),
            pltpu.VMEM((rows, cols), F32),
            pltpu.SemaphoreType.DMA((8,)),
            pltpu.SemaphoreType.DMA,
        ],
        compiler_params=pltpu.CompilerParams(vmem_limit_bytes=BUSY),
        cost_estimate=pl.CostEstimate(
            flops=2 * rows * width * cols, bytes_accessed=2 * width * cols, transcendentals=0
        ),
        name="forward",
    )(normed, gen_full, gen_head)


def store_slice(grad_values, weights_ref, row, col, out_ref):
    rows, cols = out_ref.shape[1], grad_values.shape[1]
    col = pl.ds(pl.multiple_of(col * cols, cols), cols)
    parts = 2
    deep = rows // parts
    for i in range(parts):
        at = pl.ds(pl.multiple_of(row * rows + i * deep, deep), deep)
        out_ref[:, i * deep : (i + 1) * deep] = lax.dot_general(
            grad_values, weights_ref[at, col], NT, preferred_element_type=F32
        ).astype(BF16)


def critic_kernel(
    width,
    place_ref,
    tsteps_ref,
    mix_ref,
    weight_ref,
    parts_ref,
    noise_ref,
    gram_ref,
    matrix_ref,
    head_ref,
    gen_head_ref,
    slope_ref,
    weights_ref,
    latent_ref,
    mixed_ref,
    sent_ref,
    kept_ref,
):
    level = tsteps_ref[place_ref[0]]
    parts = parts_ref[...].astype(F32)
    parts = parts[0] + parts[1] + parts[2] + parts[3]
    latent_width = latent_ref.shape[1]
    latent = parts[:, :latent_width].astype(BF16)
    latent_ref[...] = latent
    noise = noise_ref[...].astype(F32)
    noise = noise[0] + noise[1] + noise[2] + noise[3]
    noisy = mix_ref[0, level] * latent.astype(F32) + mix_ref[1, level] * noise
    noisy = noisy.astype(BF16)
    exact = noisy.astype(F32)
    rows = noisy.shape[0]
    scales = []
    turned = jnp.dot(
        exact, gram_ref[...], precision=lax.Precision.HIGHEST, preferred_element_type=F32
    )
    for which in range(2):
        own = turned[:, which * latent_width : (which + 1) * latent_width]
        square = jnp.sum(own * exact, axis=1, keepdims=True) / width
        scales.append(lax.rsqrt(jnp.maximum(square, 0.0) + 1e-06))
    wide = 256
    count = matrix_ref.shape[1] // wide
    gap = jnp.zeros((rows, latent_width), F32)
    for i in range(count):
        at = slice(i * wide, (i + 1) * wide)
        own = jnp.dot(noisy, matrix_ref[:, at], preferred_element_type=F32)
        act = twice_gelu(own * scales[i * 2 // count]).astype(BF16)
        gap = gap + lax.dot_general(act, head_ref[:, at], NT, preferred_element_type=F32)
    cotangent = (weight_ref[0, level] * (0.5 * gap)).astype(BF16)
    cot = cotangent.astype(F32)
    mixed_ref[...] = jnp.sum(cot * parts[:, latent_width:], axis=1, keepdims=True)
    grad_act = jnp.dot(cotangent, gen_head_ref[...], preferred_element_type=F32)
    grad_values = (slope_ref[...] * grad_act).astype(BF16)
    for i in range(2):
        row, col = place_ref[1 + 2 * i], place_ref[2 + 2 * i]
        store_slice(grad_values, weights_ref, row, col, sent_ref.at[i])
    for i in range(2):
        row, col = place_ref[5 + 2 * i], place_ref[6 + 2 * i]
        store_slice(grad_values, weights_ref, row, col, kept_ref.at[i])


def critics(width, place, tables, parts, own_noise, gram, matrix, head, gen_head, slope, gen_full):
    rows, cols = slope.shape
    latent_width = gen_head.shape[0]
    columns = gen_full.shape[0] // 2
    smem = pl.BlockSpec(memory_space=pltpu.SMEM)
    vmem = pl.BlockSpec(memory_space=pltpu.VMEM)
    return pl.pallas_call(
        functools.partial(critic_kernel, width),
        in_specs=[smem] * 4 + [vmem] * 8,
        out_specs=[vmem] * 4,
        out_shape=[
            jax.ShapeDtypeStruct((rows, latent_width), BF16),
            jax.ShapeDtypeStruct((rows, 1), F32),
            jax.ShapeDtypeStruct((2, rows, columns), BF16),
            jax.ShapeDtypeStruct((2, rows, columns), BF16),
        ],
        compiler_params=pltpu.CompilerParams(vmem_limit_bytes=BUSY),
        name="critics",
    )(place, *tables, parts, own_noise, gram, matrix, head, gen_head, slope, gen_full)


def finish_kernel(near_ref, far_ref, inverse_ref, gain_ref, out_ref):
    far = far_ref[...].astype(F32) * (inverse_ref[...] * gain_ref[...])
    out_ref[...] = (near_ref[...] + far).astype(BF16)


def finish(near, far, inverse, gain):
    rows, columns = near.shape
    steps = 2
    part = pl.BlockSpec((rows // steps, columns), lambda i: (i, 0))
    return pl.pallas_call(
        finish_kernel,
        grid=(steps,),
        in_specs=[
            part,
            part,
            pl.BlockSpec((rows // steps, 1), lambda i: (i, 0)),
            whole(1, columns),
        ],
        out_specs=part,
        out_shape=jax.ShapeDtypeStruct((rows, columns), BF16),
        compiler_params=pltpu.CompilerParams(vmem_limit_bytes=16 * 2**20),
        name="finish",
    )(near, far, inverse, gain)


def side_by_side_kernel(first_ref, second_ref, first_out, second_out):
    count, _, wide = first_ref.shape
    for i in range(count):
        first_out[:, i * wide : (i + 1) * wide] = first_ref[i]
        second_out[:, i * wide : (i + 1) * wide] = second_ref[i]


def side_by_side(first, second):
    count, rows, wide = first.shape
    vmem = pl.BlockSpec(memory_space=pltpu.VMEM)
    return pl.pallas_call(
        side_by_side_kernel,
        in_specs=[vmem, vmem],
        out_specs=[vmem, vmem],
        out_shape=[jax.ShapeDtypeStruct((rows, count * wide), BF16)] * 2,
        compiler_params=pltpu.CompilerParams(vmem_limit_bytes=BUSY),
        name="side_by_side",
    )(first, second)


def unpack_kernel(got_ref, slot_ref, noise_ref, matrix_ref):
    got = got_ref[...]
    total, lanes = got.shape
    half = lanes // 2
    rows = slot_ref.shape[0]
    at = lax.broadcasted_iota(jnp.int32, (rows, total), 1)
    holds = jnp.where(at == slot_ref[...], 1.0, 0.0).astype(BF16)
    noise_ref[...] = jnp.dot(holds, got, preferred_element_type=F32)[:, :half].astype(BF16)
    senders = total // ROWS
    count = 2 * (matrix_ref.shape[1] // half)
    row = lax.broadcasted_iota(jnp.int32, (count * senders, total), 0)
    at = lax.broadcasted_iota(jnp.int32, (count * senders, total), 1)
    piece = row // senders
    piece = jnp.where(piece < ROWS, piece, piece - ROWS + SLOTS)
    chosen = jnp.where(at == (row % senders) * ROWS + piece, 1.0, 0.0).astype(BF16)
    parts = jnp.dot(chosen, got, preferred_element_type=F32).astype(BF16)
    for k in range(count):
        channel = k // (count // 2) * senders
        col = k % (count // 2) * half
        side = half if k < ROWS else 0
        matrix_ref[channel : channel + senders, col : col + half] = parts[
            k * senders : (k + 1) * senders, side : side + half
        ]


def unpack(got, slot, cols):
    rows = slot.shape[0]
    half = got.shape[1] // 2
    vmem = pl.BlockSpec(memory_space=pltpu.VMEM)
    return pl.pallas_call(
        unpack_kernel,
        in_specs=[vmem, vmem],
        out_specs=[vmem, vmem],
        out_shape=[
            jax.ShapeDtypeStruct((rows, half), BF16),
            jax.ShapeDtypeStruct((half, cols), BF16),
        ],
        compiler_params=pltpu.CompilerParams(vmem_limit_bytes=16 * 2**20),
        name="unpack",
    )(got, slot)


def swap_all(x):
    return lax.all_to_all(x, SEQ, split_axis=0, concat_axis=0, tiled=True)


def local(
    hidden,
    norm_gain,
    gen_value,
    gen_head,
    critic_embed,
    critic_gain,
    critic_value,
    critic_head,
    noise,
    owner,
    tsteps,
    noise_mix,
    gap_weight,
):
    rows, width = hidden.shape
    latent_width = gen_head.shape[1]
    depth = gen_value.shape[0]
    seq_count = lax.axis_size(SEQ)
    group_id, seq_id = lax.axis_index("group"), lax.axis_index(SEQ)
    yl, c = lax.axis_index("y_lo"), lax.axis_index("core")
    shard_id = lax.axis_index(BLOCK)

    with jax.named_scope("gather_value"):
        gen_pair = lax.all_gather(gen_value, "y_hi", axis=1, tiled=True)
        gen_full = lax.all_gather(gen_pair, "z", axis=0, tiled=True)
        gen_full = pltpu.with_memory_space_constraint(gen_full, pltpu.HBM)

    with jax.named_scope("critic_matrix_part"):
        cols = critic_value.shape[1]
        critic_id = group_id // 2
        embed = lax.dynamic_slice(
            critic_embed, (critic_id, 0, seq_id * depth), (1, latent_width, depth)
        )[0].astype(F32)
        scale = lax.dynamic_slice(critic_gain, (critic_id, seq_id * depth), (1, depth))
        part = jnp.dot(
            embed * scale.astype(F32),
            critic_value.astype(F32),
            precision=lax.Precision.HIGHEST,
        )
        quarter = LANES // 2
        wide = cols // quarter
        part = part.reshape(2, seq_count, wide, quarter).transpose(1, 2, 0, 3)
        part = part.reshape(seq_count, wide, LANES).astype(BF16)

    with jax.named_scope("noise_requests"):
        crit_rows = noise.shape[0]
        target = owner // crit_rows
        at = (target[:, None] == jnp.arange(seq_count, dtype=jnp.int32)[None, :]).astype(BF16)
        ids = jnp.arange(rows, dtype=jnp.int32)
        before = (ids[None, :] < ids[:, None]).astype(BF16)
        prefix = jnp.dot(before, at, preferred_element_type=F32)
        rank = jnp.sum(prefix * at.astype(F32), axis=1, keepdims=True).astype(jnp.int32)
        mine_here = rank // SLOTS == yl * 2 + c
        slot = jnp.where(mine_here, target[:, None] * SLOTS + rank % SLOTS, -1)
        place_back = jnp.where(mine_here, target[:, None] * ROWS + rank % SLOTS, -1)
        total = seq_count * SLOTS
        holds = jnp.arange(total, dtype=jnp.int32)[:, None] == slot[:, 0][None, :]
        wanted = jnp.sum(jnp.where(holds, (owner % crit_rows + 1)[None, :], 0), axis=1)
        wanted = wanted.reshape(seq_count, SLOTS)
        digits = [jnp.pad(d, ((0, 0), (0, quarter - SLOTS))) for d in (wanted // 32, wanted % 32)]
        digits = jnp.concatenate(digits, axis=1).astype(BF16)[:, None, :]

    with jax.named_scope("first_exchange"):
        sent = jnp.concatenate([part, digits], axis=1)
        sent = jnp.pad(sent, ((0, 0), (0, 8 - sent.shape[1]), (0, 0)))
        gram = lax.dot_general(
            critic_embed, critic_embed, (((2,), (2,)), ((0,), (0,))), preferred_element_type=F32
        )
        gram = jnp.concatenate([gram[0], gram[1]], axis=1)
        got, gram = lax.optimization_barrier((swap_all(sent), gram))

    with jax.named_scope("noise_replies"):
        digits = got[:, wide].astype(F32)
        asked = (digits[:, :SLOTS] * 32 + digits[:, quarter : quarter + SLOTS]).reshape(total)
        take = asked[:, None] == jnp.arange(1, crit_rows + 1, dtype=jnp.int32).astype(F32)[None, :]
        found = jnp.dot(take.astype(BF16), noise, preferred_element_type=F32).astype(BF16)
        found = found.reshape(seq_count, SLOTS, latent_width)
        mine = jnp.sum(got[:, :wide].astype(F32), axis=0).astype(BF16)
        mine = jnp.concatenate([mine[:, :quarter], mine[:, quarter:]], axis=0)
        left = jnp.pad(mine[ROWS:], ((0, ROWS - SLOTS - (mine.shape[0] - ROWS)), (0, 0)))

    with jax.named_scope("second_exchange"):
        left = jnp.broadcast_to(left[None], (seq_count, ROWS - SLOTS, quarter))
        right = jnp.broadcast_to(mine[None, :ROWS], (seq_count, ROWS, quarter))
        sent = jnp.concatenate([jnp.concatenate([found, left], axis=1), right], axis=2)
        got = swap_all(sent)
        own_noise, matrix = unpack(got.reshape(seq_count * ROWS, LANES), place_back, cols)

    with jax.named_scope("critic_gather"):
        noise_parts = lax.all_gather(own_noise, TP, axis=0)
        matrices = lax.all_gather(matrix, ("group",) + TP, axis=0)
        head = jnp.where(critic_id == 1, critic_head, -critic_head).T
        heads = lax.all_gather(head, ("group",) + TP, axis=0)
        matrix, head = side_by_side(matrices, heads)

    with jax.named_scope("forward"):
        inputs = hidden.astype(F32)
        inverse = lax.rsqrt(jnp.mean(inputs * inputs, axis=-1, keepdims=True) + 1e-06)
        normed = (inputs * inverse * norm_gain.astype(F32)).astype(BF16)
        head_turned = gen_head.T
        head_kept = pltpu.with_memory_space_constraint(head_turned, pltpu.HBM)
        slope, part, gen_full = forward(normed, gen_full, head_kept)
        parts = lax.all_gather(part, TP, axis=0)

    with jax.named_scope("critics"):
        frame = shard_id * rows // FTOK
        place = jnp.stack([frame, 1 - c, 1 - yl, 1 - c, yl, c, 1 - yl, c, yl]).astype(jnp.int32)
        tables = (tsteps, noise_mix, gap_weight[None, :])
        gen_latent, mixed, sent, kept = critics(
            width,
            place,
            tables,
            parts,
            noise_parts,
            gram,
            matrix,
            head,
            head_turned,
            slope,
            gen_full,
        )

    with jax.named_scope("backward"):
        columns = width // 4
        first = (yl * 2 + c) * columns
        gain = lax.dynamic_slice_in_dim(norm_gain, first, columns, 0).astype(F32)
        own = lax.dynamic_slice_in_dim(hidden, first, columns, 1).astype(F32)
        slope_out = inverse * gain[None, :]
        pulled = inverse * inverse * (mixed / width)
        got = lax.ppermute(sent, "core", SWAP)
        far = (kept[0].astype(F32) + got[0].astype(F32)).astype(BF16)
        far, kept, got = lax.optimization_barrier((far, kept, got))
        far = lax.ppermute(far, "y_lo", SWAP)
        near = kept[1].astype(F32) + got[1].astype(F32)
        near = slope_out * near - own * pulled
        grad_hidden = finish(near, far, inverse, gain[None, :])
    return (gen_latent, grad_hidden)


def solution(mesh):
    shape = mesh.devices.shape
    fine = Mesh(
        mesh.devices.reshape(shape[0], 2, shape[1] // 2, 2, shape[2] // 2),
        ("group", "y_hi", "z", "y_lo", "core"),
    )
    return jax.shard_map(
        local,
        mesh=fine,
        in_specs=(
            P(BLOCK, None),
            P(),
            P(SEQ, TP),
            P(TP, None),
            P(),
            P(),
            P(SEQ, ("group",) + TP),
            P(("group",) + TP, None),
            P(SEQ, None),
            P(BLOCK),
            P(),
            P(),
            P(),
        ),
        out_specs=(P(BLOCK, None), P(BLOCK, TP)),
        check_vma=False,
    )
```

```python
import functools

import jax
import jax.numpy as jnp
from jax import lax
from jax.experimental import pallas as pl
from jax.experimental.pallas import tpu as pltpu
from jax.sharding import Mesh
from jax.sharding import PartitionSpec as P

FTOK = 2048
SLOTS = 4
ROWS = 8
LANES = 128
F32 = jnp.float32
BF16 = jnp.bfloat16
SEQ = ("y_hi", "z")
TP = ("y_lo", "core")
BLOCK = ("group",) + SEQ
SWAP = ((0, 1), (1, 0))


BUSY = 16 * 2**20
GELU_IN = 0.7978845608028654
GELU_CUBE = 0.044715
NT = (((1,), (1,)), ((), ()))


def twice_gelu(v):
    return v * (1.0 + jnp.tanh(v * (GELU_IN + (GELU_IN * GELU_CUBE) * (v * v))))


def whole(*shape):
    return pl.BlockSpec(shape, lambda *_: (0,) * len(shape))


def fetch(source, held, sems):
    count = sems.shape[0]
    deep = held.shape[0] // count
    copies = []
    for i in range(count):
        at = pl.ds(i * deep, deep)
        copies.append(pltpu.make_async_copy(source.at[at], held.at[at], sems.at[i]))
        copies[i].start()
    return copies


def forward_kernel(
    normed_ref,
    weights_ref,
    head_ref,
    slope_ref,
    part_ref,
    held,
    head_held,
    total,
    sems,
    head_sem,
):
    copies = fetch(weights_ref, held, sems)
    head_copy = pltpu.make_async_copy(head_ref, head_held, head_sem)
    head_copy.start()
    steps = 4
    each = len(copies) // steps
    half, cols = held.shape[0], total.shape[1]
    deep = half // steps
    for step in range(steps):
        for copy in copies[step * each : (step + 1) * each]:
            copy.wait()
        first = slice(step * deep, (step + 1) * deep)
        second = slice(half + step * deep, half + (step + 1) * deep)
        term = jnp.dot(normed_ref[:, first], held[first, :cols], preferred_element_type=F32)
        term += jnp.dot(normed_ref[:, second], held[first, cols:], preferred_element_type=F32)
        if step == 0:
            total[...] = term
        else:
            total[...] += term
    v = total[...]
    square = v * v
    tanh = jnp.tanh(v * (GELU_IN + (GELU_IN * GELU_CUBE) * square))
    cdf = 0.5 + 0.5 * tanh
    bend = v * (1.0 - tanh * tanh) * (0.5 * GELU_IN + (1.5 * GELU_IN * GELU_CUBE) * square)
    slope = cdf + bend
    slope_ref[...] = slope
    head_copy.wait()
    head = head_held[...]
    width = head.shape[0]
    part_ref[:, :width] = lax.dot_general(
        (v * cdf).astype(BF16), head, NT, preferred_element_type=F32
    ).astype(BF16)
    part_ref[:, width:] = lax.dot_general(
        (v * slope).astype(BF16), head, NT, preferred_element_type=F32
    ).astype(BF16)


def forward(normed, gen_full, gen_head):
    rows, width = normed.shape
    latent_width, cols = gen_head.shape
    vmem = pl.BlockSpec(memory_space=pltpu.VMEM)
    hbm = pl.BlockSpec(memory_space=pltpu.HBM)
    return pl.pallas_call(
        forward_kernel,
        in_specs=[vmem, hbm, hbm],
        out_specs=[vmem] * 3,
        out_shape=[
            jax.ShapeDtypeStruct((rows, cols), F32),
            jax.ShapeDtypeStruct((rows, 2 * latent_width), BF16),
            jax.ShapeDtypeStruct(gen_full.shape, BF16),
        ],
        scratch_shapes=[
            pltpu.VMEM(gen_head.shape, BF16),
            pltpu.VMEM((rows, cols), F32),
            pltpu.SemaphoreType.DMA((8,)),
            pltpu.SemaphoreType.DMA,
        ],
        compiler_params=pltpu.CompilerParams(vmem_limit_bytes=BUSY),
        cost_estimate=pl.CostEstimate(
            flops=2 * rows * width * cols, bytes_accessed=2 * width * cols, transcendentals=0
        ),
        name="forward",
    )(normed, gen_full, gen_head)


def store_slice(grad_values, weights_ref, row, col, out_ref):
    rows, cols = out_ref.shape[1], grad_values.shape[1]
    col = pl.ds(pl.multiple_of(col * cols, cols), cols)
    parts = 2
    deep = rows // parts
    for i in range(parts):
        at = pl.ds(pl.multiple_of(row * rows + i * deep, deep), deep)
        out_ref[:, i * deep : (i + 1) * deep] = lax.dot_general(
            grad_values, weights_ref[at, col], NT, preferred_element_type=F32
        ).astype(BF16)


def critic_kernel(
    width,
    place_ref,
    tsteps_ref,
    mix_ref,
    weight_ref,
    parts_ref,
    noise_ref,
    gram_ref,
    matrix_ref,
    head_ref,
    gen_head_ref,
    slope_ref,
    weights_ref,
    latent_ref,
    mixed_ref,
    sent_ref,
    other_ref,
    kept_ref,
):
    level = tsteps_ref[place_ref[0]]
    parts = parts_ref[...].astype(F32)
    parts = parts[0] + parts[1] + parts[2] + parts[3]
    latent_width = latent_ref.shape[1]
    latent = parts[:, :latent_width].astype(BF16)
    latent_ref[...] = latent
    noise = noise_ref[...].astype(F32)
    noise = noise[0] + noise[1] + noise[2] + noise[3]
    noisy = mix_ref[0, level] * latent.astype(F32) + mix_ref[1, level] * noise
    noisy = noisy.astype(BF16)
    exact = noisy.astype(F32)
    rows = noisy.shape[0]
    scales = []
    turned = jnp.dot(
        exact, gram_ref[...], precision=lax.Precision.HIGHEST, preferred_element_type=F32
    )
    for which in range(2):
        own = turned[:, which * latent_width : (which + 1) * latent_width]
        square = jnp.sum(own * exact, axis=1, keepdims=True) / width
        scales.append(lax.rsqrt(jnp.maximum(square, 0.0) + 1e-06))
    wide = 256
    count = matrix_ref.shape[1] // wide
    gap = jnp.zeros((rows, latent_width), F32)
    for i in range(count):
        at = slice(i * wide, (i + 1) * wide)
        own = jnp.dot(noisy, matrix_ref[:, at], preferred_element_type=F32)
        act = twice_gelu(own * scales[i * 2 // count]).astype(BF16)
        gap = gap + lax.dot_general(act, head_ref[:, at], NT, preferred_element_type=F32)
    cotangent = (weight_ref[0, level] * (0.5 * gap)).astype(BF16)
    cot = cotangent.astype(F32)
    mixed_ref[...] = jnp.sum(cot * parts[:, latent_width:], axis=1, keepdims=True)
    grad_act = jnp.dot(cotangent, gen_head_ref[...], preferred_element_type=F32)
    grad_values = (slope_ref[...] * grad_act).astype(BF16)
    for i, out_ref in enumerate((sent_ref, other_ref)):
        row, col = place_ref[1 + 2 * i], place_ref[2 + 2 * i]
        store_slice(grad_values, weights_ref, row, col, out_ref)
    for i in range(2):
        row, col = place_ref[5 + 2 * i], place_ref[6 + 2 * i]
        store_slice(grad_values, weights_ref, row, col, kept_ref.at[i])


def critics(width, place, tables, parts, own_noise, gram, matrix, head, gen_head, slope, gen_full):
    rows, cols = slope.shape
    latent_width = gen_head.shape[0]
    columns = gen_full.shape[0] // 2
    smem = pl.BlockSpec(memory_space=pltpu.SMEM)
    vmem = pl.BlockSpec(memory_space=pltpu.VMEM)
    return pl.pallas_call(
        functools.partial(critic_kernel, width),
        in_specs=[smem] * 4 + [vmem] * 8,
        out_specs=[vmem] * 5,
        out_shape=[
            jax.ShapeDtypeStruct((rows, latent_width), BF16),
            jax.ShapeDtypeStruct((rows, 1), F32),
            jax.ShapeDtypeStruct((rows, columns), BF16),
            jax.ShapeDtypeStruct((rows, columns), BF16),
            jax.ShapeDtypeStruct((2, rows, columns), BF16),
        ],
        compiler_params=pltpu.CompilerParams(vmem_limit_bytes=BUSY),
        name="critics",
    )(place, *tables, parts, own_noise, gram, matrix, head, gen_head, slope, gen_full)


def finish_kernel(near_ref, far_ref, inverse_ref, gain_ref, out_ref):
    far = far_ref[...].astype(F32) * (inverse_ref[...] * gain_ref[...])
    out_ref[...] = (near_ref[...] + far).astype(BF16)


def finish(near, far, inverse, gain):
    rows, columns = near.shape
    steps = 2
    part = pl.BlockSpec((rows // steps, columns), lambda i: (i, 0))
    return pl.pallas_call(
        finish_kernel,
        grid=(steps,),
        in_specs=[
            part,
            part,
            pl.BlockSpec((rows // steps, 1), lambda i: (i, 0)),
            whole(1, columns),
        ],
        out_specs=part,
        out_shape=jax.ShapeDtypeStruct((rows, columns), BF16),
        compiler_params=pltpu.CompilerParams(vmem_limit_bytes=16 * 2**20),
        name="finish",
    )(near, far, inverse, gain)


def side_by_side_kernel(first_ref, second_ref, first_out, second_out):
    count, _, wide = first_ref.shape
    for i in range(count):
        first_out[:, i * wide : (i + 1) * wide] = first_ref[i]
        second_out[:, i * wide : (i + 1) * wide] = second_ref[i]


def side_by_side(first, second):
    count, rows, wide = first.shape
    vmem = pl.BlockSpec(memory_space=pltpu.VMEM)
    return pl.pallas_call(
        side_by_side_kernel,
        in_specs=[vmem, vmem],
        out_specs=[vmem, vmem],
        out_shape=[jax.ShapeDtypeStruct((rows, count * wide), BF16)] * 2,
        compiler_params=pltpu.CompilerParams(vmem_limit_bytes=BUSY),
        name="side_by_side",
    )(first, second)


def unpack_kernel(got_ref, slot_ref, noise_ref, matrix_ref):
    got = got_ref[...]
    total, lanes = got.shape
    half = lanes // 2
    rows = slot_ref.shape[0]
    at = lax.broadcasted_iota(jnp.int32, (rows, total), 1)
    holds = jnp.where(at == slot_ref[...], 1.0, 0.0).astype(BF16)
    noise_ref[...] = jnp.dot(holds, got, preferred_element_type=F32)[:, :half].astype(BF16)
    senders = total // ROWS
    count = 2 * (matrix_ref.shape[1] // half)
    row = lax.broadcasted_iota(jnp.int32, (count * senders, total), 0)
    at = lax.broadcasted_iota(jnp.int32, (count * senders, total), 1)
    piece = row // senders
    piece = jnp.where(piece < ROWS, piece, piece - ROWS + SLOTS)
    chosen = jnp.where(at == (row % senders) * ROWS + piece, 1.0, 0.0).astype(BF16)
    parts = jnp.dot(chosen, got, preferred_element_type=F32).astype(BF16)
    for k in range(count):
        channel = k // (count // 2) * senders
        col = k % (count // 2) * half
        side = half if k < ROWS else 0
        matrix_ref[channel : channel + senders, col : col + half] = parts[
            k * senders : (k + 1) * senders, side : side + half
        ]


def unpack(got, slot, cols):
    rows = slot.shape[0]
    half = got.shape[1] // 2
    vmem = pl.BlockSpec(memory_space=pltpu.VMEM)
    return pl.pallas_call(
        unpack_kernel,
        in_specs=[vmem, vmem],
        out_specs=[vmem, vmem],
        out_shape=[
            jax.ShapeDtypeStruct((rows, half), BF16),
            jax.ShapeDtypeStruct((half, cols), BF16),
        ],
        compiler_params=pltpu.CompilerParams(vmem_limit_bytes=16 * 2**20),
        name="unpack",
    )(got, slot)


def swap_all(x):
    return lax.all_to_all(x, SEQ, split_axis=0, concat_axis=0, tiled=True)


def local(
    hidden,
    norm_gain,
    gen_value,
    gen_head,
    critic_embed,
    critic_gain,
    critic_value,
    critic_head,
    noise,
    owner,
    tsteps,
    noise_mix,
    gap_weight,
):
    rows, width = hidden.shape
    latent_width = gen_head.shape[1]
    depth = gen_value.shape[0]
    seq_count = lax.axis_size(SEQ)
    group_id, seq_id = lax.axis_index("group"), lax.axis_index(SEQ)
    yl, c = lax.axis_index("y_lo"), lax.axis_index("core")
    shard_id = lax.axis_index(BLOCK)

    with jax.named_scope("gather_value"):
        gen_pair = lax.all_gather(gen_value, "y_hi", axis=1, tiled=True)
        gen_full = lax.all_gather(gen_pair, "z", axis=0, tiled=True)
        gen_full = pltpu.with_memory_space_constraint(gen_full, pltpu.HBM)

    with jax.named_scope("critic_matrix_part"):
        cols = critic_value.shape[1]
        critic_id = group_id // 2
        embed = lax.dynamic_slice(
            critic_embed, (critic_id, 0, seq_id * depth), (1, latent_width, depth)
        )[0].astype(F32)
        scale = lax.dynamic_slice(critic_gain, (critic_id, seq_id * depth), (1, depth))
        part = jnp.dot(
            embed * scale.astype(F32),
            critic_value.astype(F32),
            precision=lax.Precision.HIGHEST,
        )
        quarter = LANES // 2
        wide = cols // quarter
        part = part.reshape(2, seq_count, wide, quarter).transpose(1, 2, 0, 3)
        part = part.reshape(seq_count, wide, LANES).astype(BF16)

    with jax.named_scope("noise_requests"):
        crit_rows = noise.shape[0]
        target = owner // crit_rows
        at = (target[:, None] == jnp.arange(seq_count, dtype=jnp.int32)[None, :]).astype(BF16)
        ids = jnp.arange(rows, dtype=jnp.int32)
        before = (ids[None, :] < ids[:, None]).astype(BF16)
        prefix = jnp.dot(before, at, preferred_element_type=F32)
        rank = jnp.sum(prefix * at.astype(F32), axis=1, keepdims=True).astype(jnp.int32)
        mine_here = rank // SLOTS == yl * 2 + c
        slot = jnp.where(mine_here, target[:, None] * SLOTS + rank % SLOTS, -1)
        place_back = jnp.where(mine_here, target[:, None] * ROWS + rank % SLOTS, -1)
        total = seq_count * SLOTS
        holds = jnp.arange(total, dtype=jnp.int32)[:, None] == slot[:, 0][None, :]
        wanted = jnp.sum(jnp.where(holds, (owner % crit_rows + 1)[None, :], 0), axis=1)
        wanted = wanted.reshape(seq_count, SLOTS)
        digits = [jnp.pad(d, ((0, 0), (0, quarter - SLOTS))) for d in (wanted // 32, wanted % 32)]
        digits = jnp.concatenate(digits, axis=1).astype(BF16)[:, None, :]

    with jax.named_scope("first_exchange"):
        sent = jnp.concatenate([part, digits], axis=1)
        sent = jnp.pad(sent, ((0, 0), (0, 8 - sent.shape[1]), (0, 0)))
        gram = lax.dot_general(
            critic_embed, critic_embed, (((2,), (2,)), ((0,), (0,))), preferred_element_type=F32
        )
        gram = jnp.concatenate([gram[0], gram[1]], axis=1)
        got, gram = lax.optimization_barrier((swap_all(sent), gram))

    with jax.named_scope("noise_replies"):
        digits = got[:, wide].astype(F32)
        asked = (digits[:, :SLOTS] * 32 + digits[:, quarter : quarter + SLOTS]).reshape(total)
        take = asked[:, None] == jnp.arange(1, crit_rows + 1, dtype=jnp.int32).astype(F32)[None, :]
        found = jnp.dot(take.astype(BF16), noise, preferred_element_type=F32).astype(BF16)
        found = found.reshape(seq_count, SLOTS, latent_width)
        mine = jnp.sum(got[:, :wide].astype(F32), axis=0).astype(BF16)
        mine = jnp.concatenate([mine[:, :quarter], mine[:, quarter:]], axis=0)
        left = jnp.pad(mine[ROWS:], ((0, ROWS - SLOTS - (mine.shape[0] - ROWS)), (0, 0)))

    with jax.named_scope("second_exchange"):
        left = jnp.broadcast_to(left[None], (seq_count, ROWS - SLOTS, quarter))
        right = jnp.broadcast_to(mine[None, :ROWS], (seq_count, ROWS, quarter))
        sent = jnp.concatenate([jnp.concatenate([found, left], axis=1), right], axis=2)
        got = swap_all(sent)
        own_noise, matrix = unpack(got.reshape(seq_count * ROWS, LANES), place_back, cols)

    with jax.named_scope("critic_gather"):
        noise_parts = lax.all_gather(own_noise, TP, axis=0)
        matrices = lax.all_gather(matrix, ("group",) + TP, axis=0)
        head = jnp.where(critic_id == 1, critic_head, -critic_head).T
        heads = lax.all_gather(head, ("group",) + TP, axis=0)
        matrix, head = side_by_side(matrices, heads)

    with jax.named_scope("forward"):
        inputs = hidden.astype(F32)
        inverse = lax.rsqrt(jnp.mean(inputs * inputs, axis=-1, keepdims=True) + 1e-06)
        normed = (inputs * inverse * norm_gain.astype(F32)).astype(BF16)
        head_turned = gen_head.T
        head_kept = pltpu.with_memory_space_constraint(head_turned, pltpu.HBM)
        slope, part, gen_full = forward(normed, gen_full, head_kept)
        parts = lax.all_gather(part, TP, axis=0)

    with jax.named_scope("critics"):
        frame = shard_id * rows // FTOK
        place = jnp.stack([frame, 1 - c, 1 - yl, 1 - c, yl, c, 1 - yl, c, yl]).astype(jnp.int32)
        tables = (tsteps, noise_mix, gap_weight[None, :])
        gen_latent, mixed, sent, other, kept = critics(
            width,
            place,
            tables,
            parts,
            noise_parts,
            gram,
            matrix,
            head,
            head_turned,
            slope,
            gen_full,
        )

    with jax.named_scope("backward"):
        columns = width // 4
        first = (yl * 2 + c) * columns
        gain = lax.dynamic_slice_in_dim(norm_gain, first, columns, 0).astype(F32)
        own = lax.dynamic_slice_in_dim(hidden, first, columns, 1).astype(F32)
        slope_out = inverse * gain[None, :]
        pulled = inverse * inverse * (mixed / width)
        got = lax.ppermute(sent, "core", SWAP)
        other = lax.ppermute(other, "core", SWAP)
        far = (kept[0].astype(F32) + got.astype(F32)).astype(BF16)
        far, kept = lax.optimization_barrier((far, kept))
        far = lax.ppermute(far, "y_lo", SWAP)
        near = kept[1].astype(F32) + other.astype(F32)
        near = slope_out * near - own * pulled
        grad_hidden = finish(near, far, inverse, gain[None, :])
    return (gen_latent, grad_hidden)


def solution(mesh):
    shape = mesh.devices.shape
    fine = Mesh(
        mesh.devices.reshape(shape[0], 2, shape[1] // 2, 2, shape[2] // 2),
        ("group", "y_hi", "z", "y_lo", "core"),
    )
    return jax.shard_map(
        local,
        mesh=fine,
        in_specs=(
            P(BLOCK, None),
            P(),
            P(SEQ, TP),
            P(TP, None),
            P(),
            P(),
            P(SEQ, ("group",) + TP),
            P(("group",) + TP, None),
            P(SEQ, None),
            P(BLOCK),
            P(),
            P(),
            P(),
        ),
        out_specs=(P(BLOCK, None), P(BLOCK, TP)),
        check_vma=False,
    )
```
